256 devices in a mesh: seg: 16 (over z, core), tok: 16 (over x, y).
Axes of the slice: x: 4, y: 4, z: 8, core: 2. Of those that a mesh axis runs over, the one named last changes fastest.
Arguments:
- queries: bfloat16 [2, 16, 2, 20480, 256], P(None, 'seg', None, 'tok'), may hold values from -6 to 6
- key_vectors: bfloat16 [2, 16, 2, 20480, 256], P(None, 'seg', None, 'tok'), may hold values from -6 to 6
- values: bfloat16 [2, 16, 2, 20480, 256], P(None, 'seg', None, 'tok'), may hold values from -6 to 6
- token_rates: float32 [2, 16, 2, 20480], P(None, 'seg', None, 'tok'), may hold values from 0.05 to 3
- fast_weights: float32 [16, 3, 256, 256], P('seg', None, None, 'tok'), may hold values from -0.375 to 0.375
- momenta: float32 [16, 3, 256, 256], P('seg', None, None, 'tok'), may hold values from -3 to 3
- fresh_weights: float32 [3, 256, 256], P(None, None, 'tok'), may hold values from -0.375 to 0.375
- fresh_momenta: float32 [3, 256, 256], P(None, None, 'tok'), may hold values from -3 to 3
Outputs:
- outputs: bfloat16 [2, 16, 2, 20480, 256], P(None, 'seg', None, 'tok')
- final_weights: float32 [16, 3, 256, 256], P('seg', None, None, 'tok')
- final_momenta: float32 [16, 3, 256, 256], P('seg', None, None, 'tok')
The draws below stay inside these ranges and needn't reach their ends.
All inputs are finite; a program needn't handle non-finite values.
Results may differ from the reference program's by a relative error of at most 0.033.
Values may be sent and summed in bfloat16 or wider, within the bound.
No kernel may reach another device: no remote copies, remote signals or barrier semaphores. Data moves between devices by JAX's collectives and lax.ppermute only.
A program may use at most 64 MiB of HBM per device.

```python
import math
import jax
import jax.numpy as jnp
from jax import lax

HEAD = 256
GROUPS = 2
STEPS = 2
SEGS = 16
GROUP = 20480


def draw_token_rates(key, part):
    shape = (STEPS, SEGS, GROUPS, GROUP)
    level = jnp.exp(jax.random.uniform(key, shape, jnp.float32, math.log(0.05), 0.0))
    ramp = 1.0 + 2.0 * jnp.arange(GROUP, dtype=jnp.float32) / GROUP
    return level * ramp


def block_levels(stream_key, extent, shards, least, top_value):
    level = 1.0
    for dim, blocks in shards:
        draws = jax.random.uniform(jax.random.fold_in(jax.random.fold_in(stream_key, 6), dim), (blocks,), jnp.float32, least / len(shards), top_value / len(shards))
        level = level * jnp.repeat(jnp.exp(draws), extent[dim] // blocks).reshape((-1,) + (1,) * (len(extent) - 1 - dim))
    return level


def normal_values(key, shape, scale, reach, pieces=(), kind=jnp.bfloat16):
    values = jax.random.normal(key, shape, jnp.float32) * scale
    if len(pieces) > 0:
        values = block_levels(key, shape, pieces, -0.22, 0.18) * values
    return jnp.clip(values, min=-reach, max=reach).astype(kind)


def setup_inputs(seed: int = 0) -> dict:
    arg_keys = jax.random.split(jax.random.key(seed), 9)
    queries = normal_values(arg_keys[0], (STEPS, SEGS, GROUPS, GROUP, HEAD), 1.0, 6.0, ((1, 16), (3, 16)))
    key_vectors = normal_values(arg_keys[1], (STEPS, SEGS, GROUPS, GROUP, HEAD), 1.0, 6.0, ((1, 16), (3, 16)))
    values = normal_values(arg_keys[2], (STEPS, SEGS, GROUPS, GROUP, HEAD), 1.0, 6.0, ((1, 16), (3, 16)))
    token_rates = draw_token_rates(jax.random.fold_in(arg_keys[8], 71), 0)
    fast_weights = normal_values(arg_keys[4], (SEGS, 3, HEAD, HEAD), HEAD ** -0.5, 0.375, ((0, 16), (3, 16)), jnp.float32)
    momenta = normal_values(arg_keys[5], (SEGS, 3, HEAD, HEAD), 0.5, 3.0, ((0, 16), (3, 16)), jnp.float32)
    fresh_weights = normal_values(arg_keys[6], (3, HEAD, HEAD), HEAD ** -0.5, 0.375, ((2, 16),), jnp.float32)
    fresh_momenta = normal_values(arg_keys[7], (3, HEAD, HEAD), 0.5, 3.0, ((2, 16),), jnp.float32)
    return {"queries": queries, "key_vectors": key_vectors, "values": values, "token_rates": token_rates, "fast_weights": fast_weights, "momenta": momenta, "fresh_weights": fresh_weights, "fresh_momenta": fresh_momenta}


momentum_decay = 0.9
learn_rate = 0.05
epsilon = 1e-06

def silu_parts(pre_gate):
    sigmoid_gate = jax.nn.sigmoid(pre_gate)
    return (pre_gate * sigmoid_gate, sigmoid_gate * (1.0 + pre_gate * (1.0 - sigmoid_gate)))

def local_grads(usable_weights, key_rows, value_rows, rate_rows):
    pre_gate = jnp.dot(key_rows, usable_weights[0], preferred_element_type=jnp.float32)
    pre_up = jnp.dot(key_rows, usable_weights[2], preferred_element_type=jnp.float32)
    active, slope_gate = silu_parts(pre_gate)
    hidden = (active * pre_up).astype(jnp.bfloat16)
    scaled = (rate_rows[:, None] * value_rows.astype(jnp.float32)).astype(jnp.bfloat16)
    back_hidden = -lax.dot_general(scaled, usable_weights[1], (((1,), (1,)), ((), ())), preferred_element_type=jnp.float32)
    back_gate = (back_hidden * pre_up * slope_gate).astype(jnp.bfloat16)
    back_up = (back_hidden * active).astype(jnp.bfloat16)
    contract_rows = (((0,), (0,)), ((), ()))
    grad_gate = lax.dot_general(key_rows, back_gate, contract_rows, preferred_element_type=jnp.float32)
    grad_down = -lax.dot_general(hidden, scaled, contract_rows, preferred_element_type=jnp.float32)
    grad_up = lax.dot_general(key_rows, back_up, contract_rows, preferred_element_type=jnp.float32)
    return (jnp.stack([grad_gate, grad_down, grad_up]), jnp.sum(rate_rows * rate_rows))

def update(weights, moment, gradients, rate_total):
    moment = momentum_decay * moment + gradients * lax.rsqrt(rate_total)
    stepped = weights - learn_rate * moment
    rescale = jnp.sqrt(lax.optimization_barrier(jnp.sum(weights * weights, axis=1, keepdims=True)) / (lax.optimization_barrier(jnp.sum(stepped * stepped, axis=1, keepdims=True)) + epsilon))
    return (stepped * rescale, moment)

def apply_fast(usable_weights, query_rows):
    pre_gate = jnp.dot(query_rows, usable_weights[0], preferred_element_type=jnp.float32)
    pre_up = jnp.dot(query_rows, usable_weights[2], preferred_element_type=jnp.float32)
    hidden = (jax.nn.silu(pre_gate) * pre_up).astype(jnp.bfloat16)
    return jnp.dot(hidden, usable_weights[1], preferred_element_type=jnp.float32).astype(jnp.bfloat16)

def run_segment(inputs):
    weights, moment, query_seg, key_seg, value_seg, rate_seg = inputs
    results = []
    for block_index in range(GROUPS):
        usable_weights = weights.astype(jnp.bfloat16)
        gradients, square = local_grads(usable_weights, key_seg[block_index], value_seg[block_index], rate_seg[block_index])
        weights, moment = update(weights, moment, gradients, square)
        results.append(apply_fast(weights.astype(jnp.bfloat16), query_seg[block_index]))
    return (weights, moment, jnp.stack(results))

def reference(queries, key_vectors, values, token_rates, fast_weights, momenta, fresh_weights, fresh_momenta):
    leave_weights, leave_moment, outputs_first = lax.map(run_segment, (fast_weights, momenta, queries[0], key_vectors[0], values[0], token_rates[0]))
    enter_weights = jnp.concatenate([fresh_weights[None], leave_weights[:-1]], axis=0)
    enter_moment = jnp.concatenate([fresh_momenta[None], leave_moment[:-1]], axis=0)
    final_weights, final_momenta, outputs_second = lax.map(run_segment, (enter_weights, enter_moment, queries[1], key_vectors[1], values[1], token_rates[1]))
    return (jnp.stack([outputs_first, outputs_second]), final_weights, final_momenta)
```

```python
import functools

import jax
import jax.numpy as jnp
from jax import lax
from jax.experimental import pallas as pl
from jax.experimental.pallas import tpu as pltpu
from jax.sharding import Mesh
from jax.sharding import PartitionSpec as P

TOK = ("tok_0", "tok_1")

momentum_decay = 0.9
learn_rate = 0.05
epsilon = 1e-06

f32, bf16 = jnp.float32, jnp.bfloat16
VMEM_LIMIT = 24 * 1024 * 1024

NN = (((1,), (0,)), ((), ()))
NT = (((1,), (1,)), ((), ()))


def dot(a, b, dims):
    return lax.dot_general(a, b, dims, preferred_element_type=f32)


def sigmoid(a):
    return 0.5 * jnp.tanh(0.5 * a) + 0.5


def matrix(gathered_ref, index, share):
    tiles = gathered_ref[:, index * share : (index + 1) * share, :]
    return tiles.reshape(-1, tiles.shape[-1])


def whole(*shape):
    return pl.BlockSpec(shape, lambda *_: (0,) * len(shape))


def params(**more):
    return pltpu.CompilerParams(vmem_limit_bytes=VMEM_LIMIT, **more)


def spread_kernel(weights_ref, message_ref):
    message_ref[...] = jnp.broadcast_to(weights_ref[...].astype(bf16)[None], message_ref.shape)


def spread(weights, parties):
    rows, width = weights.shape
    return pl.pallas_call(
        spread_kernel,
        out_shape=jax.ShapeDtypeStruct((parties, rows, width), bf16),
        compiler_params=params(),
        name="spread",
    )(weights)


def grads_kernel(block, tile, gathered_ref, rate_ref, key_ref, value_ref, message_ref, left_ref, acc_ref):
    parties, _, width = message_ref.shape
    share = width // parties
    step = pl.program_id(0)

    @pl.when(step == 0)
    def _():
        left_ref[...] = matrix(gathered_ref, 1, share).astype(f32).T.astype(bf16)
        acc_ref[...] = jnp.zeros_like(acc_ref)

    keys, values = key_ref[...], value_ref[...]
    rate = rate_ref[block : block + 1, pl.ds(pl.multiple_of(step * tile, tile), tile)]
    pre_gate = dot(matrix(gathered_ref, 0, share), keys, NT)
    pre_up = dot(matrix(gathered_ref, 2, share), keys, NT)
    back = dot(left_ref[...], values, NT) * -rate
    sig = sigmoid(pre_gate)
    active = pre_gate * sig
    slope = sig + active * (1.0 - sig)
    back_up = (back * active).astype(bf16)
    back_gate = (back * pre_up * slope).astype(bf16)
    hidden = (active * pre_up * rate).astype(bf16)
    acc_ref[0] += dot(back_gate, keys, NN)
    acc_ref[1] += dot(hidden, values, NN)
    acc_ref[2] += dot(back_up, keys, NN)

    @pl.when(step == pl.num_programs(0) - 1)
    def _():
        grads = (acc_ref[0], -acc_ref[1].T, acc_ref[2])
        for index, grad in enumerate(grads):
            message_ref[:, index * share : (index + 1) * share, :] = (
                grad.astype(bf16).reshape(parties, share, width)
            )
        rates = rate_ref[block : block + 1, :]
        square = jnp.sum(rates * rates, axis=1, keepdims=True)
        high = square.astype(bf16).astype(f32)
        row = lax.broadcasted_iota(jnp.int32, (share, width), 0)
        extra = jnp.where(row == 0, high, jnp.where(row == 1, square - high, 0.0))
        message_ref[:, 3 * share :, :] = jnp.broadcast_to(
            extra.astype(bf16)[None], (parties, share, width)
        )


def grads(gathered, rates, keys, values, wave_step, block):
    parties, rows, width = gathered.shape
    blocks, count = keys.shape[2], keys.shape[3]
    tile = 256
    rows_of = pl.BlockSpec(
        (None, None, None, tile, width), lambda i: (wave_step, 0, block, i, 0)
    )
    return pl.pallas_call(
        functools.partial(grads_kernel, wave_step * blocks + block, tile),
        grid=(count // tile,),
        in_specs=[whole(*gathered.shape), whole(*rates.shape), rows_of, rows_of],
        out_specs=whole(parties, rows + rows // 3, width),
        out_shape=jax.ShapeDtypeStruct((parties, rows + rows // 3, width), bf16),
        scratch_shapes=[pltpu.VMEM((width, width), bf16), pltpu.VMEM((3, width, width), f32)],
        compiler_params=params(),
        cost_estimate=pl.CostEstimate(
            flops=12 * count * width * width, bytes_accessed=4 * count * width, transcendentals=0
        ),
        name="grads",
    )(gathered, rates, keys, values)


def update_kernel(arrived_ref, weights_ref, moment_ref, new_weights_ref, new_moment_ref, message_ref, *packed):
    rows = weights_ref.shape[0]
    gradients = jnp.sum(arrived_ref[:, :rows, :].astype(f32), axis=0)
    square = jnp.sum(jnp.sum(arrived_ref[:, rows:, :].astype(f32), axis=0), axis=0, keepdims=True)
    weights = weights_ref[...]
    moment = momentum_decay * moment_ref[...] + gradients * lax.rsqrt(square)
    stepped = weights - learn_rate * moment
    rescale = jnp.sqrt(
        jnp.sum(weights * weights, axis=1, keepdims=True)
        / (jnp.sum(stepped * stepped, axis=1, keepdims=True) + epsilon)
    )
    weights = stepped * rescale
    new_weights_ref[...] = weights
    new_moment_ref[...] = moment
    rounded = weights.astype(bf16)
    message_ref[...] = jnp.broadcast_to(rounded[None], message_ref.shape)
    if packed:
        packed[0][:rows, :] = rounded
        packed[0][rows:, :] = moment.astype(bf16)


def update(arrived, weights, moment, pack):
    rows, width = weights.shape
    state = jax.ShapeDtypeStruct((rows, width), f32)
    out_shape = [state, state, jax.ShapeDtypeStruct((arrived.shape[0], rows, width), bf16)]
    if pack:
        out_shape.append(jax.ShapeDtypeStruct((2 * rows, width), bf16))
    return pl.pallas_call(
        update_kernel, out_shape=out_shape, compiler_params=params(), name="update"
    )(arrived, weights, moment)


def enter_kernel(first_ref, passed_ref, fresh_weights_ref, fresh_moment_ref, weights_ref, moment_ref, message_ref):
    rows = weights_ref.shape[0]
    first = first_ref[0] == 1
    passed = passed_ref[...].astype(f32)
    weights = jnp.where(first, fresh_weights_ref[...], passed[:rows])
    weights_ref[...] = weights
    moment_ref[...] = jnp.where(first, fresh_moment_ref[...], passed[rows:])
    message_ref[...] = jnp.broadcast_to(weights.astype(bf16)[None], message_ref.shape)


def enter(first, passed, fresh_weights, fresh_moment, parties):
    rows, width = fresh_weights.shape
    state = jax.ShapeDtypeStruct((rows, width), f32)
    vmem = pl.BlockSpec(memory_space=pltpu.VMEM)
    return pl.pallas_call(
        enter_kernel,
        in_specs=[pl.BlockSpec(memory_space=pltpu.SMEM), vmem, vmem, vmem],
        out_shape=[state, state, jax.ShapeDtypeStruct((parties, rows, width), bf16)],
        compiler_params=params(),
        name="enter",
    )(first, passed, fresh_weights, fresh_moment)


def apply_kernel(gathered_ref, query_ref, *refs):
    result_ref = refs[-1]
    share = gathered_ref.shape[1] // 3
    queries = query_ref[...]
    pre_gate = dot(queries, matrix(gathered_ref, 0, share), NT)
    pre_up = dot(queries, matrix(gathered_ref, 2, share), NT)
    hidden = (pre_gate * sigmoid(pre_gate) * pre_up).astype(bf16)
    result_ref[...] = dot(hidden, matrix(gathered_ref, 1, share), NT).astype(bf16)


def apply_fast(gathered, queries, results, wave_step, block):
    count, width = queries.shape[3:]
    tile = 256
    rows_of = pl.BlockSpec(
        (None, None, None, tile, width), lambda i: (wave_step, 0, block, i, 0)
    )
    given = [gathered, queries]
    in_specs = [whole(*gathered.shape), rows_of]
    if results is not None:
        given.append(results)
        in_specs.append(pl.BlockSpec(memory_space=pl.ANY))
    return pl.pallas_call(
        apply_kernel,
        grid=(count // tile,),
        in_specs=in_specs,
        out_specs=rows_of,
        out_shape=jax.ShapeDtypeStruct(queries.shape, bf16),
        input_output_aliases={} if results is None else {2: 0},
        compiler_params=params(),
        cost_estimate=pl.CostEstimate(
            flops=6 * count * width * width, bytes_accessed=4 * count * width, transcendentals=0
        ),
        name="apply",
    )(*given)


def exchanged(tiles):
    return lax.all_to_all(tiles, TOK, split_axis=0, concat_axis=0, tiled=True)


def passed_on(array):
    length = lax.axis_size("seg")
    return lax.ppermute(array, "seg", [(i, i + 1) for i in range(length - 1)])


def columns_first(state):
    return jnp.swapaxes(state, 1, 2).reshape(-1, state.shape[1])


def rows_first(state, share):
    return jnp.swapaxes(state.reshape(-1, share, state.shape[1]), 1, 2)


def body(
    queries, key_vectors, values, token_rates, fast_weights, momenta, fresh_weights, fresh_momenta
):
    sections, _, blocks, count, _ = queries.shape
    parties = lax.axis_size(TOK)
    share = fast_weights.shape[3]
    rates = token_rates.reshape(sections * blocks, count)
    first = (lax.axis_index("seg") == 0).astype(jnp.int32).reshape(1)
    weights, moment = columns_first(fast_weights[0]), columns_first(momenta[0])
    fresh_weights, fresh_moment = columns_first(fresh_weights), columns_first(fresh_momenta)
    gathered = exchanged(spread(weights, parties))
    results = None
    for wave_step in range(sections):
        for block in range(blocks):
            leaving = block == blocks - 1 and wave_step < sections - 1
            arrived = exchanged(grads(gathered, rates, key_vectors, values, wave_step, block))
            weights, moment, message, *packed = update(arrived, weights, moment, leaving)
            gathered = exchanged(message)
            results = apply_fast(gathered, queries, results, wave_step, block)
            if leaving:
                weights, moment, message = enter(
                    first, passed_on(packed[0]), fresh_weights, fresh_moment, parties
                )
                gathered = exchanged(message)
    return (results, rows_first(weights, share)[None], rows_first(moment, share)[None])


def solution(mesh):
    finer = Mesh(mesh.devices.reshape(mesh.shape["seg"], 4, 4), ("seg", "tok_0", "tok_1"))
    placed = (
        P(None, "seg", None, TOK, None),
        P(None, "seg", None, TOK, None),
        P(None, "seg", None, TOK, None),
        P(None, "seg", None, TOK),
        P("seg", None, None, TOK),
        P("seg", None, None, TOK),
        P(None, None, TOK),
        P(None, None, TOK),
    )
    return jax.shard_map(
        body,
        mesh=finer,
        in_specs=placed,
        out_specs=(
            P(None, "seg", None, TOK, None),
            P("seg", None, None, TOK),
            P("seg", None, None, TOK),
        ),
        check_vma=False,
    )
```

```python
import functools

import jax
import jax.numpy as jnp
from jax import lax
from jax.experimental import pallas as pl
from jax.experimental.pallas import tpu as pltpu
from jax.sharding import Mesh
from jax.sharding import PartitionSpec as P

TOK = ("tok_0", "tok_1")

momentum_decay = 0.9
learn_rate = 0.05
epsilon = 1e-06

f32, bf16 = jnp.float32, jnp.bfloat16
VMEM_LIMIT = 16 * 1024 * 1024

NN = (((1,), (0,)), ((), ()))
NT = (((1,), (1,)), ((), ()))


def dot(a, b, dims):
    return lax.dot_general(a, b, dims, preferred_element_type=f32)


def sigmoid(a):
    return 0.5 * jnp.tanh(0.5 * a) + 0.5


def matrix(gathered_ref, index, share):
    tiles = gathered_ref[:, index * share : (index + 1) * share, :]
    return tiles.reshape(-1, tiles.shape[-1])


def params(**more):
    return pltpu.CompilerParams(vmem_limit_bytes=VMEM_LIMIT, **more)


def in_vmem(*shape, dtype=f32):
    return pltpu.VMEM(shape, dtype)


VMEM = pl.BlockSpec(memory_space=pltpu.VMEM)
HBM = pl.BlockSpec(memory_space=pltpu.HBM)
ANY = pl.BlockSpec(memory_space=pl.ANY)
SMEM = pl.BlockSpec(memory_space=pltpu.SMEM)


TOKEN = jax.ShapeDtypeStruct((8, 128), f32)


def in_hbm(array):
    return pltpu.with_memory_space_constraint(array, pltpu.HBM)


def spread_kernel(weights_ref, message_ref, token_ref):
    message_ref[...] = jnp.broadcast_to(weights_ref[...].astype(bf16)[None], message_ref.shape)
    token_ref[...] = jnp.zeros_like(token_ref)


def spread(weights, parties):
    rows, width = weights.shape
    return pl.pallas_call(
        spread_kernel,
        in_specs=[VMEM],
        out_specs=[VMEM] * 2,
        out_shape=[in_vmem(parties, rows, width, dtype=bf16), TOKEN],
        compiler_params=params(),
        name="spread",
    )(weights)


def stage_kernel(place, count, *refs):
    sources, targets, sems = refs[1 : 1 + count], refs[1 + count : 1 + 2 * count], refs[-1]
    copies = [
        pltpu.make_async_copy(source.at[*place], target, sems.at[index])
        for index, (source, target) in enumerate(zip(sources, targets))
    ]
    for copy in copies:
        copy.start()
    for copy in copies:
        copy.wait()


def stage(token, place, *arrays):
    return pl.pallas_call(
        functools.partial(stage_kernel, place, len(arrays)),
        in_specs=[VMEM] + [HBM] * len(arrays),
        out_specs=[VMEM] * len(arrays),
        out_shape=[in_vmem(*array.shape[3:], dtype=array.dtype) for array in arrays],
        scratch_shapes=[pltpu.SemaphoreType.DMA((len(arrays),))],
        compiler_params=params(),
        cost_estimate=pl.CostEstimate(
            flops=0, bytes_accessed=len(arrays) * arrays[0].size, transcendentals=0
        ),
        name="stage",
    )(token, *(in_hbm(array) for array in arrays))


def grads_kernel(
    block, tile, offset, gathered_ref, rate_ref, key_rows, value_rows, message_ref, left_ref, back_ref
):
    parties, rows, width = message_ref.shape
    share = width // parties
    count = key_rows.shape[0]
    base = offset // share
    left_ref[...] = matrix(gathered_ref, base + 1, share).astype(f32).T.astype(bf16)
    gate, up = matrix(gathered_ref, base, share), matrix(gathered_ref, base + 2, share)
    for start in range(0, count, tile):
        span = slice(start, start + tile)
        keys, values = key_rows[span, :], value_rows[span, :]
        rate = rate_ref[block : block + 1, span]
        pre_gate = dot(gate, keys, NT)
        pre_up = dot(up, keys, NT)
        back = dot(left_ref[...], values, NT) * -rate
        sig = sigmoid(pre_gate)
        active = pre_gate * sig
        slope = sig + active * (1.0 - sig)
        back_ref[0, :, span] = (back * pre_up * slope).astype(bf16)
        back_ref[1, :, span] = (active * pre_up * rate).astype(bf16)
        back_ref[2, :, span] = (back * active).astype(bf16)
    keys, values = key_rows[...], value_rows[...]
    gradients = (
        dot(back_ref[0], keys, NN),
        -dot(back_ref[1], values, NN).T,
        dot(back_ref[2], keys, NN),
    )
    for index, gradient in enumerate(gradients):
        message_ref[:, index * share : (index + 1) * share, :] = gradient.astype(bf16).reshape(
            parties, share, width
        )
    if rows > 3 * share:
        rates = rate_ref[...]
        squares = jnp.sum(rates * rates, axis=1, keepdims=True)
        row = lax.broadcasted_iota(jnp.int32, (share, width), 0)
        extra = jnp.zeros((share, width), f32)
        for index in range(rates.shape[0]):
            square = squares[index : index + 1, :]
            high = square.astype(bf16).astype(f32)
            extra = jnp.where(row == 2 * index, high, extra)
            extra = jnp.where(row == 2 * index + 1, square - high, extra)
        message_ref[:, 3 * share :, :] = jnp.broadcast_to(
            extra.astype(bf16)[None], (parties, share, width)
        )


def grads(gathered, offset, rates, keys, values, index):
    parties, _, width = gathered.shape
    share = width // parties
    count = keys.shape[0]
    rows = (4 if index == 0 else 3) * share
    return pl.pallas_call(
        functools.partial(grads_kernel, index, 256, offset),
        in_specs=[VMEM] * 4,
        out_specs=VMEM,
        out_shape=in_vmem(parties, rows, width, dtype=bf16),
        scratch_shapes=[pltpu.VMEM((width, width), bf16), pltpu.VMEM((3, width, count), bf16)],
        compiler_params=params(),
        cost_estimate=pl.CostEstimate(
            flops=12 * count * width * width, bytes_accessed=4 * count * width, transcendentals=0
        ),
        name="grads",
    )(gathered, rates, keys, values)


def update_kernel(index, waits, *refs):
    arrived_ref, weights_ref, moment_ref = refs[:3]
    refs = refs[3:]
    rows = weights_ref.shape[0]
    gradients = jnp.sum(arrived_ref[:, :rows, :].astype(f32), axis=0)
    if index == 0:
        squares = jnp.sum(arrived_ref[:, rows:, :].astype(f32), axis=0)
        refs[-2][...] = squares
    else:
        squares, refs = refs[0][...], refs[1:]
    new_weights_ref, new_moment_ref, message_ref = refs[waits : waits + 3]
    token_ref = refs[-1]
    token_ref[...] = jnp.zeros_like(token_ref)
    square = squares[2 * index : 2 * index + 1, :] + squares[2 * index + 1 : 2 * index + 2, :]
    weights = weights_ref[...]
    moment = momentum_decay * moment_ref[...] + gradients * lax.rsqrt(square)
    stepped = weights - learn_rate * moment
    rescale = jnp.sqrt(
        jnp.sum(weights * weights, axis=1, keepdims=True)
        / (jnp.sum(stepped * stepped, axis=1, keepdims=True) + epsilon)
    )
    weights = stepped * rescale
    new_weights_ref[...] = weights
    new_moment_ref[...] = moment
    rounded = weights.astype(bf16)
    if len(message_ref.shape) == 3:
        message_ref[...] = jnp.broadcast_to(rounded[None], message_ref.shape)
    else:
        message_ref[:rows, :] = rounded
        message_ref[rows:, :] = moment.astype(bf16)


def update(index, arrived, weights, moment, squares, token, leaving):
    rows, width = weights.shape
    given, in_specs = [arrived, weights, moment], [VMEM] * 3
    if index > 0:
        given.append(squares)
        in_specs.append(VMEM)
    if token is not None:
        given.append(token)
        in_specs.append(VMEM)
    out_shape = [in_vmem(rows, width), in_vmem(rows, width)]
    if leaving:
        out_shape.append(in_vmem(2 * rows, width, dtype=bf16))
    else:
        out_shape.append(in_vmem(arrived.shape[0], rows, width, dtype=bf16))
    if index == 0:
        out_shape.append(in_vmem(arrived.shape[1] - rows, width))
    out_shape.append(TOKEN)
    return pl.pallas_call(
        functools.partial(update_kernel, index, int(token is not None)),
        in_specs=in_specs,
        out_specs=[VMEM] * len(out_shape),
        out_shape=out_shape,
        compiler_params=params(),
        name="update",
    )(*given)


def enter_kernel(
    first_ref,
    passed_ref,
    own_ref,
    fresh_weights_ref,
    fresh_moment_ref,
    weights_ref,
    moment_ref,
    message_ref,
    token_ref,
):
    token_ref[...] = jnp.zeros_like(token_ref)
    rows = weights_ref.shape[0]
    first = first_ref[0] == 1
    passed = passed_ref[...].astype(f32)
    weights = jnp.where(first, fresh_weights_ref[...], passed[:rows])
    weights_ref[...] = weights
    moment_ref[...] = jnp.where(first, fresh_moment_ref[...], passed[rows:])
    shape = (message_ref.shape[0], *weights.shape)
    message_ref[:, :rows, :] = jnp.broadcast_to(weights.astype(bf16)[None], shape)
    message_ref[:, rows:, :] = jnp.broadcast_to(own_ref[:rows, :][None], shape)


def enter(first, passed, own, fresh_weights, fresh_moment, parties):
    rows, width = fresh_weights.shape
    return pl.pallas_call(
        enter_kernel,
        in_specs=[SMEM] + [VMEM] * 4,
        out_specs=[VMEM] * 4,
        out_shape=[
            in_vmem(rows, width),
            in_vmem(rows, width),
            in_vmem(parties, 2 * rows, width, dtype=bf16),
            TOKEN,
        ],
        compiler_params=params(),
        name="enter",
    )(first, passed, own, fresh_weights, fresh_moment)


def apply_kernel(place, offset, staged, gathered_ref, query_ref, *refs):
    out_ref, token_ref, query_rows, held_ref, sems = refs[-5:]
    token_ref[...] = jnp.zeros_like(token_ref)
    width = query_rows.shape[-1]
    share = width // gathered_ref.shape[0]
    base = offset // share
    if staged:
        queries = query_ref[...]
    else:
        copy = pltpu.make_async_copy(query_ref.at[*place], query_rows, sems.at[0])
        copy.start()
        copy.wait()
        queries = query_rows[...]
    pre_gate = dot(queries, matrix(gathered_ref, base, share), NT)
    pre_up = dot(queries, matrix(gathered_ref, base + 2, share), NT)
    hidden = (pre_gate * sigmoid(pre_gate) * pre_up).astype(bf16)
    held_ref[...] = dot(hidden, matrix(gathered_ref, base + 1, share), NT).astype(bf16)
    copy = pltpu.make_async_copy(held_ref, out_ref.at[*place], sems.at[1])
    copy.start()
    copy.wait()


def apply_fast(gathered, offset, queries, results, shape, wave_step, block):
    count, width = shape[3:]
    staged = len(queries.shape) == 2
    given, in_specs = [gathered, queries], [VMEM, VMEM if staged else HBM]
    if results is not None:
        given.append(results)
        in_specs.append(HBM)
    return pl.pallas_call(
        functools.partial(apply_kernel, (wave_step, 0, block), offset, staged),
        in_specs=in_specs,
        out_specs=[HBM, VMEM],
        out_shape=[jax.ShapeDtypeStruct(shape, bf16), TOKEN],
        input_output_aliases={} if results is None else {2: 0},
        scratch_shapes=[
            pltpu.VMEM((count, width), bf16),
            pltpu.VMEM((count, width), bf16),
            pltpu.SemaphoreType.DMA((2,)),
        ],
        compiler_params=params(),
        cost_estimate=pl.CostEstimate(
            flops=6 * count * width * width, bytes_accessed=4 * count * width, transcendentals=0
        ),
        name="apply",
    )(*given)


def exchanged(tiles):
    return lax.all_to_all(tiles, TOK, split_axis=0, concat_axis=0, tiled=True)


def passed_on(array):
    length = lax.axis_size("seg")
    return lax.ppermute(array, "seg", [(i, i + 1) for i in range(length - 1)])


def columns_first(state):
    return jnp.swapaxes(state, 1, 2).reshape(-1, state.shape[1])


def rows_first(state, share):
    return jnp.swapaxes(state.reshape(-1, share, state.shape[1]), 1, 2)


def body(
    queries, key_vectors, values, token_rates, fast_weights, momenta, fresh_weights, fresh_momenta
):
    sections, _, blocks, count, _ = queries.shape
    parties = lax.axis_size(TOK)
    share = fast_weights.shape[3]
    rates = token_rates.reshape(sections * blocks, count)
    first = (lax.axis_index("seg") == 0).astype(jnp.int32).reshape(1)
    weights, moment = columns_first(fast_weights[0]), columns_first(momenta[0])
    fresh_weights, fresh_moment = columns_first(fresh_weights), columns_first(fresh_momenta)
    message, token = spread(weights, parties)
    gathered, offset = exchanged(message), 0
    results = squares = applied = pending = None
    rows = weights.shape[0]
    for wave_step in range(sections):
        for block in range(blocks):
            index = wave_step * blocks + block
            leaving = block == blocks - 1 and wave_step < sections - 1
            rows_here = stage(token, (wave_step, 0, block), key_vectors, values)
            arrived = exchanged(grads(gathered, offset, rates, *rows_here, index))
            if pending is not None:
                results, applied = apply_fast(
                    gathered, pending[0], in_hbm(queries), results, queries.shape, *pending[1:]
                )
            weights, moment, message, *more, token = update(
                index, arrived, weights, moment, squares, applied, leaving
            )
            squares = more[0] if more else squares
            offset = 0
            pending = (0, wave_step, block)
            if leaving:
                weights, moment, message, token = enter(
                    first, passed_on(message), message, fresh_weights, fresh_moment, parties
                )
                pending = (rows, wave_step, block)
            gathered = exchanged(message)
    (last_rows,) = stage(token, (sections - 1, 0, blocks - 1), queries)
    results, _ = apply_fast(gathered, pending[0], last_rows, results, queries.shape, *pending[1:])
    return (results, rows_first(weights, share)[None], rows_first(moment, share)[None])


def solution(mesh):
    finer = Mesh(mesh.devices.reshape(mesh.shape["seg"], 4, 4), ("seg", "tok_0", "tok_1"))
    placed = (
        P(None, "seg", None, TOK, None),
        P(None, "seg", None, TOK, None),
        P(None, "seg", None, TOK, None),
        P(None, "seg", None, TOK),
        P("seg", None, None, TOK),
        P("seg", None, None, TOK),
        P(None, None, TOK),
        P(None, None, TOK),
    )
    return jax.shard_map(
        body,
        mesh=finer,
        in_specs=placed,
        out_specs=(
            P(None, "seg", None, TOK, None),
            P("seg", None, None, TOK),
            P("seg", None, None, TOK),
        ),
        check_vma=False,
    )
```

```python
import functools

import jax
import jax.numpy as jnp
from jax import lax
from jax.experimental import pallas as pl
from jax.experimental.pallas import tpu as pltpu
from jax.sharding import Mesh
from jax.sharding import PartitionSpec as P

TOK = ("tok_0", "tok_1")

momentum_decay = 0.9
learn_rate = 0.05
epsilon = 1e-06

f32, bf16 = jnp.float32, jnp.bfloat16
VMEM_LIMIT = 16 * 1024 * 1024

NN = (((1,), (0,)), ((), ()))
NT = (((1,), (1,)), ((), ()))


def dot(a, b, dims):
    return lax.dot_general(a, b, dims, preferred_element_type=f32)


def sigmoid(a):
    return 0.5 * jnp.tanh(0.5 * a) + 0.5


def matrix(gathered_ref, index, share):
    tiles = gathered_ref[:, index * share : (index + 1) * share, :]
    return tiles.reshape(-1, tiles.shape[-1])


def params(**more):
    return pltpu.CompilerParams(vmem_limit_bytes=VMEM_LIMIT, **more)


def in_vmem(*shape, dtype=f32):
    return pltpu.VMEM(shape, dtype)


VMEM = pl.BlockSpec(memory_space=pltpu.VMEM)
HBM = pl.BlockSpec(memory_space=pltpu.HBM)
SMEM = pl.BlockSpec(memory_space=pltpu.SMEM)


TOKEN = jax.ShapeDtypeStruct((8, 128), f32)


def in_hbm(array):
    return pltpu.with_memory_space_constraint(array, pltpu.HBM)


def started(sources, targets, places, sems):
    copies = [
        pltpu.make_async_copy(source.at[*place], target, sems.at[index])
        for index, (source, target, place) in enumerate(zip(sources, targets, places))
    ]
    for copy in copies:
        copy.start()
    return copies


def rows_in_vmem(array):
    return in_vmem(*array.shape[3:], dtype=array.dtype)


def stage_kernel(places, *refs):
    count = len(places)
    token_ref, sems = refs[-2:]
    copies = started(refs[1 : 1 + count], refs[1 + count : 1 + 2 * count], places, sems)
    token_ref[...] = jnp.zeros_like(token_ref)
    for copy in copies:
        copy.wait()


def stage(token, place, *arrays):
    count = len(arrays)
    return pl.pallas_call(
        functools.partial(stage_kernel, [place] * count),
        in_specs=[VMEM] + [HBM] * count,
        out_specs=[VMEM] * (count + 1),
        out_shape=[rows_in_vmem(array) for array in arrays] + [TOKEN],
        scratch_shapes=[pltpu.SemaphoreType.DMA((count,))],
        compiler_params=params(),
        cost_estimate=pl.CostEstimate(
            flops=0, bytes_accessed=count * arrays[0].size, transcendentals=0
        ),
        name="stage",
    )(token, *(in_hbm(array) for array in arrays))


def begin_kernel(place, weights_ref, key_ref, value_ref, message_ref, key_rows, value_rows, token_ref, sems):
    copies = started((key_ref, value_ref), (key_rows, value_rows), [place] * 2, sems)
    message_ref[...] = jnp.broadcast_to(weights_ref[...].astype(bf16)[None], message_ref.shape)
    token_ref[...] = jnp.zeros_like(token_ref)
    for copy in copies:
        copy.wait()


def begin(weights, place, keys, values, parties):
    rows, width = weights.shape
    return pl.pallas_call(
        functools.partial(begin_kernel, place),
        in_specs=[VMEM, HBM, HBM],
        out_specs=[VMEM] * 4,
        out_shape=[
            in_vmem(parties, rows, width, dtype=bf16),
            rows_in_vmem(keys),
            rows_in_vmem(values),
            TOKEN,
        ],
        scratch_shapes=[pltpu.SemaphoreType.DMA((2,))],
        compiler_params=params(),
        name="begin",
    )(weights, in_hbm(keys), in_hbm(values))


def grads_kernel(
    place, tile, gathered_ref, rate_ref, key_rows, value_rows, message_ref, token_ref, left_ref, back_ref
):
    parties, rows, width = message_ref.shape
    share = width // parties
    count = key_rows.shape[0]
    section, block = place
    token_ref[...] = jnp.zeros_like(token_ref)
    left_ref[...] = matrix(gathered_ref, 1, share).astype(f32).T.astype(bf16)
    gate, up = matrix(gathered_ref, 0, share), matrix(gathered_ref, 2, share)
    for start in range(0, count, tile):
        span = slice(start, start + tile)
        keys, values = key_rows[span, :], value_rows[span, :]
        rate = rate_ref[section, 0, block : block + 1, span]
        pre_gate = dot(gate, keys, NT)
        pre_up = dot(up, keys, NT)
        back = dot(left_ref[...], values, NT) * -rate
        sig = sigmoid(pre_gate)
        active = pre_gate * sig
        slope = sig + active * (1.0 - sig)
        back_ref[0, :, span] = (back * pre_up * slope).astype(bf16)
        back_ref[1, :, span] = (active * pre_up * rate).astype(bf16)
        back_ref[2, :, span] = (back * active).astype(bf16)
    keys, values = key_rows[...], value_rows[...]
    gradients = (
        dot(back_ref[0], keys, NN),
        -dot(back_ref[1], values, NN).T,
        dot(back_ref[2], keys, NN),
    )
    for index, gradient in enumerate(gradients):
        message_ref[:, index * share : (index + 1) * share, :] = gradient.astype(bf16).reshape(
            parties, share, width
        )
    if rows > 3 * share:
        row = lax.broadcasted_iota(jnp.int32, (share, width), 0)
        extra = jnp.zeros((share, width), f32)
        blocks = rate_ref.shape[2]
        for index in range(rate_ref.shape[0] * blocks):
            each = index % blocks
            rates = rate_ref[index // blocks, 0, each : each + 1, :]
            square = jnp.sum(rates * rates, axis=1, keepdims=True)
            high = square.astype(bf16).astype(f32)
            extra = jnp.where(row == 2 * index, high, extra)
            extra = jnp.where(row == 2 * index + 1, square - high, extra)
        message_ref[:, 3 * share :, :] = jnp.broadcast_to(
            extra.astype(bf16)[None], (parties, share, width)
        )


def grads(gathered, rates, keys, values, place):
    parties, _, width = gathered.shape
    share = width // parties
    count = keys.shape[0]
    rows = (4 if place == (0, 0) else 3) * share
    return pl.pallas_call(
        functools.partial(grads_kernel, place, 256),
        in_specs=[VMEM] * 4,
        out_specs=[VMEM] * 2,
        out_shape=[in_vmem(parties, rows, width, dtype=bf16), TOKEN],
        scratch_shapes=[pltpu.VMEM((width, width), bf16), pltpu.VMEM((3, width, count), bf16)],
        compiler_params=params(),
        cost_estimate=pl.CostEstimate(
            flops=12 * count * width * width, bytes_accessed=4 * count * width, transcendentals=0
        ),
        name="grads",
    )(gathered, rates, keys, values)


def update_kernel(index, *refs):
    arrived_ref, weights_ref, moment_ref = refs[:3]
    refs = refs[3:]
    rows = weights_ref.shape[0]
    gradients = jnp.sum(arrived_ref[:, :rows, :].astype(f32), axis=0)
    if index == 0:
        squares = jnp.sum(arrived_ref[:, rows:, :].astype(f32), axis=0)
        refs[-1][...] = squares
    else:
        squares, refs = refs[0][...], refs[1:]
    square = squares[2 * index : 2 * index + 1, :] + squares[2 * index + 1 : 2 * index + 2, :]
    weights = weights_ref[...]
    moment = momentum_decay * moment_ref[...] + gradients * lax.rsqrt(square)
    stepped = weights - learn_rate * moment
    rescale = jnp.sqrt(
        jnp.sum(weights * weights, axis=1, keepdims=True)
        / (jnp.sum(stepped * stepped, axis=1, keepdims=True) + epsilon)
    )
    weights = stepped * rescale
    rounded = weights.astype(bf16)
    message_ref = refs[1]
    if len(message_ref.shape) == 3:
        message_ref[...] = jnp.broadcast_to(rounded[None], message_ref.shape)
        refs[2][...] = weights
        refs[3][...] = moment
    else:
        message_ref[:rows, :] = rounded
        message_ref[rows:, :] = moment.astype(bf16)


def update(index, arrived, weights, moment, squares, token, leaving):
    rows, width = weights.shape
    given, in_specs = [arrived, weights, moment], [VMEM] * 3
    if index > 0:
        given.append(squares)
        in_specs.append(VMEM)
    given.append(token)
    in_specs.append(VMEM)
    if leaving:
        out_shape = [in_vmem(2 * rows, width, dtype=bf16)]
    else:
        out_shape = [in_vmem(arrived.shape[0], rows, width, dtype=bf16)]
        out_shape += [in_vmem(rows, width)] * 2
    if index == 0:
        out_shape.append(in_vmem(arrived.shape[1] - rows, width))
    return pl.pallas_call(
        functools.partial(update_kernel, index),
        in_specs=in_specs,
        out_specs=[VMEM] * len(out_shape),
        out_shape=out_shape,
        compiler_params=params(),
        name="update",
    )(*given)


def enter_kernel(
    first_ref, passed_ref, own_ref, fresh_weights_ref, fresh_moment_ref, weights_ref, moment_ref, message_ref
):
    rows = weights_ref.shape[0]
    first = first_ref[0] == 1
    passed = passed_ref[...].astype(f32)
    weights = jnp.where(first, fresh_weights_ref[...], passed[:rows])
    weights_ref[...] = weights
    moment_ref[...] = jnp.where(first, fresh_moment_ref[...], passed[rows:])
    shape = (message_ref.shape[0], *weights.shape)
    message_ref[:, :rows, :] = jnp.broadcast_to(weights.astype(bf16)[None], shape)
    message_ref[:, rows:, :] = jnp.broadcast_to(own_ref[:rows, :][None], shape)


def enter(first, passed, own, fresh_weights, fresh_moment, parties):
    rows, width = fresh_weights.shape
    return pl.pallas_call(
        enter_kernel,
        in_specs=[SMEM] + [VMEM] * 4,
        out_specs=[VMEM] * 3,
        out_shape=[
            in_vmem(rows, width),
            in_vmem(rows, width),
            in_vmem(parties, 2 * rows, width, dtype=bf16),
        ],
        compiler_params=params(),
        name="enter",
    )(first, passed, own, fresh_weights, fresh_moment)


def apply_kernel(place, base, ahead, staged, aliased, gathered_ref, query_ref, *refs):
    count = len(ahead)
    sources, refs = refs[:count], refs[count + aliased :]
    out_ref, token_ref, targets = refs[0], refs[1], refs[2 : 2 + count]
    query_rows, held_ref, sems = refs[2 + count :]
    token_ref[...] = jnp.zeros_like(token_ref)
    share = query_rows.shape[-1] // gathered_ref.shape[0]
    copies = []
    if not staged:
        copies += started([query_ref], [query_rows], [place], sems)
    copies += started(sources, targets, ahead, sems.at[pl.ds(2, max(count, 1))])
    if staged:
        queries = query_ref[...]
    else:
        copies.pop(0).wait()
        queries = query_rows[...]
    pre_gate = dot(queries, matrix(gathered_ref, base + 0, share), NT)
    pre_up = dot(queries, matrix(gathered_ref, base + 2, share), NT)
    hidden = (pre_gate * sigmoid(pre_gate) * pre_up).astype(bf16)
    held_ref[...] = dot(hidden, matrix(gathered_ref, base + 1, share), NT).astype(bf16)
    copies.append(pltpu.make_async_copy(held_ref, out_ref.at[*place], sems.at[1]))
    copies[-1].start()
    for copy in copies:
        copy.wait()


def apply_fast(gathered, base, queries, place, results, shape, ahead=()):
    count, width = shape[3:]
    staged = len(queries.shape) == 2
    given = [gathered, queries if staged else in_hbm(queries)]
    given += [in_hbm(array) for array, _ in ahead]
    in_specs = [VMEM, VMEM if staged else HBM] + [HBM] * len(ahead)
    if results is not None:
        given.append(results)
        in_specs.append(HBM)
    return pl.pallas_call(
        functools.partial(
            apply_kernel, place, base, [where for _, where in ahead], staged, int(results is not None)
        ),
        in_specs=in_specs,
        out_specs=[HBM] + [VMEM] * (1 + len(ahead)),
        out_shape=[jax.ShapeDtypeStruct(shape, bf16), TOKEN]
        + [rows_in_vmem(array) for array, _ in ahead],
        input_output_aliases={} if results is None else {len(given) - 1: 0},
        scratch_shapes=[
            pltpu.VMEM((count, width), bf16),
            pltpu.VMEM((count, width), bf16),
            pltpu.SemaphoreType.DMA((2 + max(len(ahead), 1),)),
        ],
        compiler_params=params(),
        cost_estimate=pl.CostEstimate(
            flops=6 * count * width * width, bytes_accessed=4 * count * width, transcendentals=0
        ),
        name="apply",
    )(*given)


def exchanged(tiles):
    return lax.all_to_all(tiles, TOK, split_axis=0, concat_axis=0, tiled=True)


def passed_on(array):
    length = lax.axis_size("seg")
    return lax.ppermute(array, "seg", [(i, i + 1) for i in range(length - 1)])


def columns_first(state):
    return jnp.swapaxes(state, 1, 2).reshape(-1, state.shape[1])


def rows_first(state, share):
    return jnp.swapaxes(state.reshape(-1, share, state.shape[1]), 1, 2)


def body(
    queries, key_vectors, values, token_rates, fast_weights, momenta, fresh_weights, fresh_momenta
):
    sections, _, blocks, count, _ = queries.shape
    parties = lax.axis_size(TOK)
    share = fast_weights.shape[3]
    first = (lax.axis_index("seg") == 0).astype(jnp.int32).reshape(1)
    weights, moment = columns_first(fast_weights[0]), columns_first(momenta[0])
    fresh_weights, fresh_moment = columns_first(fresh_weights), columns_first(fresh_momenta)
    shape = queries.shape
    places = [(section, 0, block) for section in range(sections) for block in range(blocks)]
    message, *staged, _ = begin(weights, places[0], key_vectors, values, parties)
    gathered, base = exchanged(message), 0
    results = squares = None
    for index, place in enumerate(places):
        last = index == len(places) - 1
        leaving = not last and place[2] == blocks - 1
        message, token = grads(gathered, token_rates, *staged, (place[0], place[2]))
        arrived = exchanged(message)
        if last:
            ahead = ((queries, place),)
        else:
            ahead = ((key_vectors, places[index + 1]), (values, places[index + 1]))
        if index == 0:
            *staged, token = stage(token, ahead[0][1], *(array for array, _ in ahead))
        else:
            results, token, *staged = apply_fast(
                gathered, base, queries, places[index - 1], results, shape, ahead
            )
        message, *state = update(index, arrived, weights, moment, squares, token, leaving)
        base = 0
        if leaving:
            weights, moment, message = enter(
                first, passed_on(message), message, fresh_weights, fresh_moment, parties
            )
            base = 3
        else:
            weights, moment, squares = (*state, squares)[:3]
        gathered = exchanged(message)
    results, *_ = apply_fast(gathered, base, staged[0], places[-1], results, shape)
    return (results, rows_first(weights, share)[None], rows_first(moment, share)[None])


def solution(mesh):
    finer = Mesh(mesh.devices.reshape(mesh.shape["seg"], 4, 4), ("seg", "tok_0", "tok_1"))
    placed = (
        P(None, "seg", None, TOK, None),
        P(None, "seg", None, TOK, None),
        P(None, "seg", None, TOK, None),
        P(None, "seg", None, TOK),
        P("seg", None, None, TOK),
        P("seg", None, None, TOK),
        P(None, None, TOK),
        P(None, None, TOK),
    )
    return jax.shard_map(
        body,
        mesh=finer,
        in_specs=placed,
        out_specs=(
            P(None, "seg", None, TOK, None),
            P("seg", None, None, TOK),
            P("seg", None, None, TOK),
        ),
        check_vma=False,
    )
```

```python
import functools

import jax
import jax.numpy as jnp
from jax import lax
from jax.experimental import pallas as pl
from jax.experimental.pallas import tpu as pltpu
from jax.sharding import Mesh
from jax.sharding import PartitionSpec as P

TOK = ("tok_0", "tok_1")

momentum_decay = 0.9
learn_rate = 0.05
epsilon = 1e-06

f32, bf16 = jnp.float32, jnp.bfloat16
VMEM_LIMIT = 16 * 1024 * 1024

NN = (((1,), (0,)), ((), ()))
NT = (((1,), (1,)), ((), ()))


def dot(a, b, dims):
    return lax.dot_general(a, b, dims, preferred_element_type=f32)


def sigmoid(a):
    return 0.5 * jnp.tanh(0.5 * a) + 0.5


def matrix(gathered_ref, index, share):
    tiles = gathered_ref[:, index * share : (index + 1) * share, :]
    return tiles.reshape(-1, tiles.shape[-1])


def params(**more):
    return pltpu.CompilerParams(vmem_limit_bytes=VMEM_LIMIT, **more)


def in_vmem(*shape, dtype=f32):
    return pltpu.VMEM(shape, dtype)


VMEM = pl.BlockSpec(memory_space=pltpu.VMEM)
HBM = pl.BlockSpec(memory_space=pltpu.HBM)
SMEM = pl.BlockSpec(memory_space=pltpu.SMEM)


TOKEN = jax.ShapeDtypeStruct((8, 128), f32)


def in_hbm(array):
    return pltpu.with_memory_space_constraint(array, pltpu.HBM)


def started(sources, targets, places, sems):
    copies = [
        pltpu.make_async_copy(source.at[*place], target, sems.at[index])
        for index, (source, target, place) in enumerate(zip(sources, targets, places))
    ]
    for copy in copies:
        copy.start()
    return copies


def rows_in_vmem(array):
    return in_vmem(*array.shape[3:], dtype=array.dtype)


def spread_kernel(weights_ref, message_ref, token_ref, held_ref, sem):
    copy = pltpu.make_async_copy(weights_ref, held_ref, sem)
    copy.start()
    token_ref[...] = jnp.zeros_like(token_ref)
    copy.wait()
    message_ref[...] = jnp.broadcast_to(held_ref[...].astype(bf16)[None], message_ref.shape)


def spread(weights, parties):
    rows, width = weights.shape
    return pl.pallas_call(
        spread_kernel,
        in_specs=[HBM],
        out_specs=[VMEM] * 2,
        out_shape=[in_vmem(parties, rows, width, dtype=bf16), TOKEN],
        scratch_shapes=[pltpu.VMEM((rows, width), f32), pltpu.SemaphoreType.DMA],
        compiler_params=params(),
        name="spread",
    )(in_hbm(weights))


def stage_kernel(places, *refs):
    count = len(places)
    token_ref, sems = refs[-2:]
    copies = started(refs[1 : 1 + count], refs[-2 - count : -2], places, sems)
    token_ref[...] = jnp.zeros_like(token_ref)
    handed = refs[1 + count : -2 - count]
    for source, target in zip(handed[: len(handed) // 2], handed[len(handed) // 2 :]):
        target[...] = source[...]
    for copy in copies:
        copy.wait()


def stage(token, place, arrays, handed=()):
    count = len(arrays)
    return pl.pallas_call(
        functools.partial(stage_kernel, [place] * count),
        in_specs=[VMEM] + [HBM] * count + [VMEM] * len(handed),
        out_specs=[VMEM] * (len(handed) + count + 1),
        out_shape=[in_vmem(*array.shape, dtype=array.dtype) for array in handed]
        + [rows_in_vmem(array) for array in arrays]
        + [TOKEN],
        scratch_shapes=[pltpu.SemaphoreType.DMA((count,))],
        compiler_params=params(),
        cost_estimate=pl.CostEstimate(
            flops=0, bytes_accessed=count * arrays[0].size, transcendentals=0
        ),
        name="stage",
    )(token, *(in_hbm(array) for array in arrays), *handed)


def grads_kernel(
    place, tile, gathered_ref, rate_ref, key_rows, value_rows, message_ref, token_ref, left_ref, back_ref, held_ref, sems
):
    parties, rows, width = message_ref.shape
    share = width // parties
    count = key_rows.shape[0]
    section, block = place
    token_ref[...] = jnp.zeros_like(token_ref)
    left_ref[...] = matrix(gathered_ref, 1, share).astype(f32).T.astype(bf16)
    gate, up = matrix(gathered_ref, 0, share), matrix(gathered_ref, 2, share)
    for start in range(0, count, tile):
        span = slice(start, start + tile)
        keys, values = key_rows[span, :], value_rows[span, :]
        rate = rate_ref[section, 0, block : block + 1, span]
        pre_gate = dot(gate, keys, NT)
        pre_up = dot(up, keys, NT)
        back = dot(left_ref[...], values, NT) * -rate
        sig = sigmoid(pre_gate)
        active = pre_gate * sig
        slope = sig + active * (1.0 - sig)
        back_ref[0, :, span] = (back * pre_up * slope).astype(bf16)
        back_ref[1, :, span] = (active * pre_up * rate).astype(bf16)
        back_ref[2, :, span] = (back * active).astype(bf16)
    copies = []

    def send(index, tiles):
        part = pl.ds(index * share, share)
        held_ref[:, index * share : (index + 1) * share, :] = tiles
        copies.append(
            pltpu.make_async_copy(
                held_ref.at[:, part, :], message_ref.at[:, part, :], sems.at[index]
            )
        )
        copies[-1].start()

    if rows > 3 * share:
        row = lax.broadcasted_iota(jnp.int32, (share, width), 0)
        extra = jnp.zeros((share, width), f32)
        blocks = rate_ref.shape[2]
        for index in range(rate_ref.shape[0] * blocks):
            each = index % blocks
            rates = rate_ref[index // blocks, 0, each : each + 1, :]
            square = jnp.sum(rates * rates, axis=1, keepdims=True)
            high = square.astype(bf16).astype(f32)
            extra = jnp.where(row == 2 * index, high, extra)
            extra = jnp.where(row == 2 * index + 1, square - high, extra)
        send(3, jnp.broadcast_to(extra.astype(bf16)[None], (parties, share, width)))
    keys, values = key_rows[...], value_rows[...]
    shape = (parties, share, width)
    send(1, -dot(back_ref[1], values, NN).T.astype(bf16).reshape(shape))
    send(0, dot(back_ref[0], keys, NN).astype(bf16).reshape(shape))
    send(2, dot(back_ref[2], keys, NN).astype(bf16).reshape(shape))
    for copy in copies:
        copy.wait()


def grads(gathered, rates, keys, values, place):
    parties, _, width = gathered.shape
    share = width // parties
    count = keys.shape[0]
    rows = (4 if place == (0, 0) else 3) * share
    return pl.pallas_call(
        functools.partial(grads_kernel, place, 256),
        in_specs=[VMEM] * 4,
        out_specs=[HBM, VMEM],
        out_shape=[jax.ShapeDtypeStruct((parties, rows, width), bf16), TOKEN],
        scratch_shapes=[
            pltpu.VMEM((width, width), bf16),
            pltpu.VMEM((3, width, count), bf16),
            pltpu.VMEM((parties, rows, width), bf16),
            pltpu.SemaphoreType.DMA((4,)),
        ],
        compiler_params=params(),
        cost_estimate=pl.CostEstimate(
            flops=12 * count * width * width, bytes_accessed=4 * count * width, transcendentals=0
        ),
        name="grads",
    )(gathered, rates, keys, values)


def update_kernel(index, *refs):
    arrived_ref, weights_ref, moment_ref = refs[:3]
    refs = refs[3:]
    rows = weights_ref.shape[0]
    gradients = jnp.sum(arrived_ref[:, :rows, :].astype(f32), axis=0)
    if index == 0:
        squares = jnp.sum(arrived_ref[:, rows:, :].astype(f32), axis=0)
        refs[-1][...] = squares
    else:
        squares, refs = refs[0][...], refs[1:]
    square = squares[2 * index : 2 * index + 1, :] + squares[2 * index + 1 : 2 * index + 2, :]
    weights = weights_ref[...]
    moment = momentum_decay * moment_ref[...] + gradients * lax.rsqrt(square)
    stepped = weights - learn_rate * moment
    rescale = jnp.sqrt(
        jnp.sum(weights * weights, axis=1, keepdims=True)
        / (jnp.sum(stepped * stepped, axis=1, keepdims=True) + epsilon)
    )
    weights = stepped * rescale
    rounded = weights.astype(bf16)
    message_ref = refs[1]
    if len(message_ref.shape) == 3:
        message_ref[...] = jnp.broadcast_to(rounded[None], message_ref.shape)
        refs[2][...] = weights
        refs[3][...] = moment
    else:
        message_ref[:rows, :] = rounded
        message_ref[rows:, :] = moment.astype(bf16)


def update(index, arrived, weights, moment, squares, token, leaving):
    rows, width = weights.shape
    given, in_specs = [arrived, weights, moment], [VMEM] * 3
    if index > 0:
        given.append(squares)
        in_specs.append(VMEM)
    given.append(token)
    in_specs.append(VMEM)
    if leaving:
        out_shape = [in_vmem(2 * rows, width, dtype=bf16)]
    else:
        out_shape = [in_vmem(arrived.shape[0], rows, width, dtype=bf16)]
        out_shape += [in_vmem(rows, width)] * 2
    if index == 0:
        out_shape.append(in_vmem(arrived.shape[1] - rows, width))
    return pl.pallas_call(
        functools.partial(update_kernel, index),
        in_specs=in_specs,
        out_specs=[VMEM] * len(out_shape),
        out_shape=out_shape,
        compiler_params=params(),
        name="update",
    )(*given)


def enter_kernel(
    first_ref, passed_ref, fresh_weights_ref, fresh_moment_ref, weights_ref, moment_ref, message_ref
):
    rows = weights_ref.shape[0]
    first = first_ref[0] == 1
    passed = passed_ref[...].astype(f32)
    weights = jnp.where(first, fresh_weights_ref[...], passed[:rows])
    weights_ref[...] = weights
    moment_ref[...] = jnp.where(first, fresh_moment_ref[...], passed[rows:])
    message_ref[...] = jnp.broadcast_to(weights.astype(bf16)[None], message_ref.shape)


def enter(first, passed, fresh_weights, fresh_moment, parties):
    rows, width = fresh_weights.shape
    return pl.pallas_call(
        enter_kernel,
        in_specs=[SMEM] + [VMEM] * 3,
        out_specs=[VMEM] * 3,
        out_shape=[
            in_vmem(rows, width),
            in_vmem(rows, width),
            in_vmem(parties, rows, width, dtype=bf16),
        ],
        compiler_params=params(),
        name="enter",
    )(first, passed, fresh_weights, fresh_moment)


def apply_kernel(place, ahead, staged, aliased, parts, chosen, gathered_ref, query_ref, wait_ref, *refs):
    count = len(ahead)
    if chosen:
        other_ref, flag_ref = refs[:2]
        refs = refs[2:]

        gathered_ref = jnp.where(flag_ref[0] == 1, other_ref[...], gathered_ref[...])

    sources, refs = refs[:count], refs[count + aliased :]
    out_ref, token_ref, targets = refs[0], refs[1], refs[2 : 2 + count]
    query_rows, held_ref, sems, ahead_sems = refs[2 + count :]
    token_ref[...] = jnp.zeros_like(token_ref)
    length, width = query_rows.shape
    share = width // gathered_ref.shape[0]
    if not staged:
        (first,) = started([query_ref], [query_rows], [place], sems.at[pl.ds(parts, 1)])
    copies = started(sources, targets, ahead, ahead_sems)
    if not staged:
        first.wait()
    rows_ref = query_ref if staged else query_rows
    size = length // parts
    for part in range(parts):
        queries = rows_ref[part * size : (part + 1) * size, :]
        pre_gate = dot(queries, matrix(gathered_ref, 0, share), NT)
        pre_up = dot(queries, matrix(gathered_ref, 2, share), NT)
        hidden = (pre_gate * sigmoid(pre_gate) * pre_up).astype(bf16)
        held_ref[part * size : (part + 1) * size, :] = dot(
            hidden, matrix(gathered_ref, 1, share), NT
        ).astype(bf16)
        span = pl.ds(part * size, size)
        copies.append(
            pltpu.make_async_copy(held_ref.at[span, :], out_ref.at[*place].at[span, :], sems.at[part])
        )
        copies[-1].start()
    for copy in copies:
        copy.wait()


def apply_fast(gathered, queries, place, results, shape, token, ahead=(), parts=1, instead=()):
    count, width = shape[3:]
    staged = len(queries.shape) == 2
    given = [gathered, queries if staged else in_hbm(queries), token]
    given += [*instead, *(in_hbm(array) for array, _ in ahead)]
    in_specs = [VMEM, VMEM if staged else HBM, VMEM]
    in_specs += [VMEM, SMEM][: len(instead)] + [HBM] * len(ahead)
    if results is not None:
        given.append(results)
        in_specs.append(HBM)
    return pl.pallas_call(
        functools.partial(
            apply_kernel,
            place,
            [where for _, where in ahead],
            staged,
            int(results is not None),
            parts,
            bool(instead),
        ),
        in_specs=in_specs,
        out_specs=[HBM] + [VMEM] * (1 + len(ahead)),
        out_shape=[jax.ShapeDtypeStruct(shape, bf16), TOKEN]
        + [rows_in_vmem(array) for array, _ in ahead],
        input_output_aliases={} if results is None else {len(given) - 1: 0},
        scratch_shapes=[
            pltpu.VMEM((count, width), bf16),
            pltpu.VMEM((count, width), bf16),
            pltpu.SemaphoreType.DMA((parts + 1,)),
            pltpu.SemaphoreType.DMA((max(len(ahead), 1),)),
        ],
        compiler_params=params(),
        cost_estimate=pl.CostEstimate(
            flops=6 * count * width * width, bytes_accessed=4 * count * width, transcendentals=0
        ),
        name="apply",
    )(*given)


def exchanged(tiles):
    return lax.all_to_all(tiles, TOK, split_axis=0, concat_axis=0, tiled=True)


def passed_on(array):
    length = lax.axis_size("seg")
    return lax.ppermute(array, "seg", [(i, i + 1) for i in range(length - 1)])


def handed_back(array):
    length = lax.axis_size("seg")
    return lax.ppermute(array, "seg", [(i + 1, i) for i in range(length - 1)])


def columns_first(state):
    return jnp.swapaxes(state, 1, 2).reshape(-1, state.shape[1])


def rows_first(state, share):
    return jnp.swapaxes(state.reshape(-1, share, state.shape[1]), 1, 2)


def body(
    queries, key_vectors, values, token_rates, fast_weights, momenta, fresh_weights, fresh_momenta
):
    sections, _, blocks, count, _ = queries.shape
    parties = lax.axis_size(TOK)
    share = fast_weights.shape[3]
    place_in_chain = lax.axis_index("seg")
    first = (place_in_chain == 0).astype(jnp.int32).reshape(1)
    is_last = place_in_chain == lax.axis_size("seg") - 1
    weights, moment = columns_first(fast_weights[0]), columns_first(momenta[0])
    fresh_weights, fresh_moment = columns_first(fresh_weights), columns_first(fresh_momenta)
    rows, shape = weights.shape[0], queries.shape
    places = [(section, 0, block) for section in range(sections) for block in range(blocks)]
    message, token = spread(weights, parties)
    *staged, _ = stage(token, places[0], (key_vectors, values))
    gathered = exchanged(message)
    results = squares = left = owed = None
    for index, place in enumerate(places):
        last = index == len(places) - 1
        leaving = not last and place[2] == blocks - 1
        message, token = grads(gathered, token_rates, *staged, (place[0], place[2]))
        arrived = exchanged(message)
        if last:
            ahead = ((queries, place),)
        else:
            ahead = ((key_vectors, places[index + 1]), (values, places[index + 1]))
        if index == 0:
            *staged, token = stage(token, places[1], (key_vectors, values))
        elif left is not None:
            handed, *staged, token = stage(
                token, places[index + 1], (key_vectors, values), (gathered,)
            )
            back = handed_back(handed)
            own = lax.cond(
                is_last,
                lambda mine: exchanged(jnp.broadcast_to(mine[None], (parties, *mine.shape))),
                lambda mine: jnp.zeros((parties, *mine.shape), bf16),
                left[:rows],
            )
            owed, left = (back, places[index - 1], own), None
        else:
            results, token, *staged = apply_fast(
                gathered, queries, places[index - 1], results, shape, token, ahead
            )
        message, *state = update(index, arrived, weights, moment, squares, token, leaving)
        if leaving:
            left = message
            weights, moment, message = enter(
                first, passed_on(message), fresh_weights, fresh_moment, parties
            )
        else:
            weights, moment, squares = (*state, squares)[:3]
        gathered = exchanged(message)
    results, token = apply_fast(
        owed[0],
        queries,
        owed[1],
        results,
        shape,
        weights,
        instead=(owed[2], is_last.astype(jnp.int32).reshape(1)),
    )
    results, _ = apply_fast(gathered, staged[0], places[-1], results, shape, token, parts=2)
    return (results, rows_first(weights, share)[None], rows_first(moment, share)[None])


def solution(mesh):
    finer = Mesh(mesh.devices.reshape(mesh.shape["seg"], 4, 4), ("seg", "tok_0", "tok_1"))
    placed = (
        P(None, "seg", None, TOK, None),
        P(None, "seg", None, TOK, None),
        P(None, "seg", None, TOK, None),
        P(None, "seg", None, TOK),
        P("seg", None, None, TOK),
        P("seg", None, None, TOK),
        P(None, None, TOK),
        P(None, None, TOK),
    )
    return jax.shard_map(
        body,
        mesh=finer,
        in_specs=placed,
        out_specs=(
            P(None, "seg", None, TOK, None),
            P("seg", None, None, TOK),
            P("seg", None, None, TOK),
        ),
        check_vma=False,
    )
```

```python
import functools

import jax
import jax.numpy as jnp
from jax import lax
from jax.experimental import pallas as pl
from jax.experimental.pallas import tpu as pltpu
from jax.sharding import Mesh
from jax.sharding import PartitionSpec as P

TOK = ("tok_0", "tok_1")

momentum_decay = 0.9
learn_rate = 0.05
epsilon = 1e-06

f32, bf16 = jnp.float32, jnp.bfloat16
VMEM_LIMIT = 16 * 1024 * 1024

NN = (((1,), (0,)), ((), ()))
NT = (((1,), (1,)), ((), ()))


def dot(a, b, dims):
    return lax.dot_general(a, b, dims, preferred_element_type=f32)


def sigmoid(a):
    return 0.5 * jnp.tanh(0.5 * a) + 0.5


def matrix(gathered_ref, index, share):
    tiles = gathered_ref[:, index * share : (index + 1) * share, :]
    return tiles.reshape(-1, tiles.shape[-1])


def params(**more):
    return pltpu.CompilerParams(vmem_limit_bytes=VMEM_LIMIT, **more)


def in_vmem(*shape, dtype=f32):
    return pltpu.VMEM(shape, dtype)


VMEM = pl.BlockSpec(memory_space=pltpu.VMEM)
HBM = pl.BlockSpec(memory_space=pltpu.HBM)
SMEM = pl.BlockSpec(memory_space=pltpu.SMEM)


TOKEN = jax.ShapeDtypeStruct((8, 128), f32)


def in_hbm(array):
    return pltpu.with_memory_space_constraint(array, pltpu.HBM)


def started(sources, targets, places, sems):
    copies = [
        pltpu.make_async_copy(source.at[*place], target, sems.at[index])
        for index, (source, target, place) in enumerate(zip(sources, targets, places))
    ]
    for copy in copies:
        copy.start()
    return copies


def rows_in_vmem(array):
    return in_vmem(*array.shape[3:], dtype=array.dtype)


def spread_kernel(weights_ref, message_ref, token_ref, held_ref, sem):
    copy = pltpu.make_async_copy(weights_ref, held_ref, sem)
    copy.start()
    token_ref[...] = jnp.zeros_like(token_ref)
    copy.wait()
    message_ref[...] = jnp.broadcast_to(held_ref[...].astype(bf16)[None], message_ref.shape)


def spread(weights, parties):
    rows, width = weights.shape
    return pl.pallas_call(
        spread_kernel,
        in_specs=[HBM],
        out_specs=[VMEM] * 2,
        out_shape=[in_vmem(parties, rows, width, dtype=bf16), TOKEN],
        scratch_shapes=[pltpu.VMEM((rows, width), f32), pltpu.SemaphoreType.DMA],
        compiler_params=params(),
        name="spread",
    )(in_hbm(weights))


def copies_kernel(state_ref, message_ref):
    rows = message_ref.shape[1]
    message_ref[...] = jnp.broadcast_to(state_ref[:rows, :][None], message_ref.shape)


def stage_kernel(places, *refs):
    count = len(places)
    token_ref, sems = refs[-2:]
    copies = started(refs[1 : 1 + count], refs[-2 - count : -2], places, sems)
    token_ref[...] = jnp.zeros_like(token_ref)
    for copy in copies:
        copy.wait()


def stage(token, place, arrays):
    count = len(arrays)
    return pl.pallas_call(
        functools.partial(stage_kernel, [place] * count),
        in_specs=[VMEM] + [HBM] * count,
        out_specs=[VMEM] * (count + 1),
        out_shape=[rows_in_vmem(array) for array in arrays] + [TOKEN],
        scratch_shapes=[pltpu.SemaphoreType.DMA((count,))],
        compiler_params=params(),
        cost_estimate=pl.CostEstimate(
            flops=0, bytes_accessed=count * arrays[0].size, transcendentals=0
        ),
        name="stage",
    )(token, *(in_hbm(array) for array in arrays))


def grads_kernel(place, tile, ahead, gathered_ref, rate_ref, key_rows, value_rows, *refs):
    later = len(ahead)
    message_ref = refs[later]
    left_ref, back_ref, sems = refs[-3:]
    copies = started(refs[:later], refs[later + 1 : 2 * later + 1], ahead, sems)
    parties, rows, width = message_ref.shape
    share = width // parties
    count = key_rows.shape[0]
    section, block = place
    left_ref[...] = matrix(gathered_ref, 1, share).astype(f32).T.astype(bf16)
    gate, up = matrix(gathered_ref, 0, share), matrix(gathered_ref, 2, share)
    for start in range(0, count, tile):
        span = slice(start, start + tile)
        keys, values = key_rows[span, :], value_rows[span, :]
        rate = rate_ref[section, 0, block : block + 1, span]
        pre_gate = dot(gate, keys, NT)
        pre_up = dot(up, keys, NT)
        back = dot(left_ref[...], values, NT) * -rate
        sig = sigmoid(pre_gate)
        active = pre_gate * sig
        slope = sig + active * (1.0 - sig)
        back_ref[0, :, span] = (back * pre_up * slope).astype(bf16)
        back_ref[1, :, span] = (active * pre_up * rate).astype(bf16)
        back_ref[2, :, span] = (back * active).astype(bf16)
    keys, values = key_rows[...], value_rows[...]
    gradients = (
        dot(back_ref[0], keys, NN),
        -dot(back_ref[1], values, NN).T,
        dot(back_ref[2], keys, NN),
    )
    for index, gradient in enumerate(gradients):
        message_ref[:, index * share : (index + 1) * share, :] = gradient.astype(bf16).reshape(
            parties, share, width
        )
    if rows > 3 * share:
        row = lax.broadcasted_iota(jnp.int32, (share, width), 0)
        extra = jnp.zeros((share, width), f32)
        blocks = rate_ref.shape[2]
        for index in range(rate_ref.shape[0] * blocks):
            each = index % blocks
            rates = rate_ref[index // blocks, 0, each : each + 1, :]
            square = jnp.sum(rates * rates, axis=1, keepdims=True)
            high = square.astype(bf16).astype(f32)
            extra = jnp.where(row == 2 * index, high, extra)
            extra = jnp.where(row == 2 * index + 1, square - high, extra)
        message_ref[:, 3 * share :, :] = jnp.broadcast_to(
            extra.astype(bf16)[None], (parties, share, width)
        )
    for copy in copies:
        copy.wait()


def grads(gathered, rates, keys, values, place, ahead):
    parties, _, width = gathered.shape
    share = width // parties
    count = keys.shape[0]
    rows = (4 if place == (0, 0) else 3) * share
    return pl.pallas_call(
        functools.partial(grads_kernel, place, 256, [where for _, where in ahead]),
        in_specs=[VMEM] * 4 + [HBM] * len(ahead),
        out_specs=[VMEM] * (1 + len(ahead)),
        out_shape=[in_vmem(parties, rows, width, dtype=bf16)]
        + [rows_in_vmem(array) for array, _ in ahead],
        scratch_shapes=[
            pltpu.VMEM((width, width), bf16),
            pltpu.VMEM((3, width, count), bf16),
            pltpu.SemaphoreType.DMA((len(ahead),)),
        ],
        compiler_params=params(),
        cost_estimate=pl.CostEstimate(
            flops=12 * count * width * width, bytes_accessed=4 * count * width, transcendentals=0
        ),
        name="grads",
    )(gathered, rates, keys, values, *(in_hbm(array) for array, _ in ahead))


def update_kernel(index, waits, *refs):
    arrived_ref, weights_ref, moment_ref = refs[:3]
    refs = refs[3:]
    rows = weights_ref.shape[0]
    gradients = jnp.sum(arrived_ref[:, :rows, :].astype(f32), axis=0)
    if index == 0:
        squares = jnp.sum(arrived_ref[:, rows:, :].astype(f32), axis=0)
        refs[-1][...] = squares
    else:
        squares, refs = refs[0][...], refs[1:]
    square = squares[2 * index : 2 * index + 1, :] + squares[2 * index + 1 : 2 * index + 2, :]
    weights = weights_ref[...]
    moment = momentum_decay * moment_ref[...] + gradients * lax.rsqrt(square)
    stepped = weights - learn_rate * moment
    rescale = jnp.sqrt(
        jnp.sum(weights * weights, axis=1, keepdims=True)
        / (jnp.sum(stepped * stepped, axis=1, keepdims=True) + epsilon)
    )
    weights = stepped * rescale
    rounded = weights.astype(bf16)
    refs = refs[waits:]
    message_ref = refs[0]
    if len(message_ref.shape) == 3:
        message_ref[...] = jnp.broadcast_to(rounded[None], message_ref.shape)
        refs[1][...] = weights
        refs[2][...] = moment
    else:
        message_ref[:rows, :] = rounded
        message_ref[rows:, :] = moment.astype(bf16)


def update(index, arrived, weights, moment, squares, token, leaving):
    rows, width = weights.shape
    given, in_specs = [arrived, weights, moment], [VMEM] * 3
    if index > 0:
        given.append(squares)
        in_specs.append(VMEM)
    waits = token is not None
    if waits:
        given.append(token)
        in_specs.append(VMEM)
    if leaving:
        out_shape = [in_vmem(2 * rows, width, dtype=bf16)]
    else:
        out_shape = [in_vmem(arrived.shape[0], rows, width, dtype=bf16)]
        out_shape += [in_vmem(rows, width)] * 2
    if index == 0:
        out_shape.append(in_vmem(arrived.shape[1] - rows, width))
    return pl.pallas_call(
        functools.partial(update_kernel, index, waits),
        in_specs=in_specs,
        out_specs=[VMEM] * len(out_shape),
        out_shape=out_shape,
        compiler_params=params(),
        name="update",
    )(*given)


def enter_kernel(
    first_ref, passed_ref, fresh_weights_ref, fresh_moment_ref, weights_ref, moment_ref, message_ref
):
    rows = weights_ref.shape[0]
    first = first_ref[0] == 1
    passed = passed_ref[...].astype(f32)
    weights = jnp.where(first, fresh_weights_ref[...], passed[:rows])
    weights_ref[...] = weights
    moment_ref[...] = jnp.where(first, fresh_moment_ref[...], passed[rows:])
    message_ref[...] = jnp.broadcast_to(weights.astype(bf16)[None], message_ref.shape)


def enter(first, passed, fresh_weights, fresh_moment, parties):
    rows, width = fresh_weights.shape
    return pl.pallas_call(
        enter_kernel,
        in_specs=[SMEM] + [VMEM] * 3,
        out_specs=[VMEM] * 3,
        out_shape=[
            in_vmem(rows, width),
            in_vmem(rows, width),
            in_vmem(parties, rows, width, dtype=bf16),
        ],
        compiler_params=params(),
        name="enter",
    )(first, passed, fresh_weights, fresh_moment)


def apply_kernel(place, staged, waits, chosen, parts, gathered_ref, query_ref, *refs):
    refs = refs[waits:]
    if chosen:
        gathered_ref = jnp.where(refs[1][0] == 1, refs[0][...], gathered_ref[...])
    out_ref, token_ref, query_rows, held_ref, sems = refs[-5:]
    token_ref[...] = jnp.zeros_like(token_ref)
    length, width = query_rows.shape
    share = width // gathered_ref.shape[0]
    if staged:
        query_rows = query_ref
    else:
        (copy,) = started([query_ref], [query_rows], [place], sems)
        copy.wait()
    size = length // parts
    copies = []
    for part in range(parts):
        queries = query_rows[part * size : (part + 1) * size, :]
        pre_gate = dot(queries, matrix(gathered_ref, 0, share), NT)
        pre_up = dot(queries, matrix(gathered_ref, 2, share), NT)
        hidden = (pre_gate * sigmoid(pre_gate) * pre_up).astype(bf16)
        held_ref[part * size : (part + 1) * size, :] = dot(
            hidden, matrix(gathered_ref, 1, share), NT
        ).astype(bf16)
        span = pl.ds(part * size, size)
        copies.append(
            pltpu.make_async_copy(
                held_ref.at[span, :], out_ref.at[*place].at[span, :], sems.at[1 + part]
            )
        )
        copies[-1].start()
    for copy in copies:
        copy.wait()


def apply_fast(gathered, queries, place, results, shape, token=None, parts=1, instead=()):
    count, width = shape[3:]
    staged = len(queries.shape) == 2
    waits = token is not None
    given = [gathered, queries if staged else in_hbm(queries)]
    in_specs = [VMEM, VMEM if staged else HBM]
    if waits:
        given.append(token)
        in_specs.append(VMEM)
    if instead:
        given += instead
        in_specs += [VMEM, SMEM]
    if results is not None:
        given.append(results)
        in_specs.append(HBM)
    return pl.pallas_call(
        functools.partial(apply_kernel, place, staged, waits, bool(instead), parts),
        in_specs=in_specs,
        out_specs=[HBM, VMEM],
        out_shape=[jax.ShapeDtypeStruct(shape, bf16), TOKEN],
        input_output_aliases={} if results is None else {len(given) - 1: 0},
        scratch_shapes=[
            pltpu.VMEM((count, width), bf16),
            pltpu.VMEM((count, width), bf16),
            pltpu.SemaphoreType.DMA((1 + parts,)),
        ],
        compiler_params=params(),
        cost_estimate=pl.CostEstimate(
            flops=6 * count * width * width, bytes_accessed=4 * count * width, transcendentals=0
        ),
        name="apply",
    )(*given)


def exchanged(tiles):
    return lax.all_to_all(tiles, TOK, split_axis=0, concat_axis=0, tiled=True)


def passed_on(array):
    length = lax.axis_size("seg")
    return lax.ppermute(array, "seg", [(i, i + 1) for i in range(length - 1)])


def handed_back(array):
    length = lax.axis_size("seg")
    return lax.ppermute(array, "seg", [(i + 1, i) for i in range(length - 1)])


def gathered_by_last(is_last, state, rows, parties):
    width = state.shape[1]
    message = pl.pallas_call(
        copies_kernel,
        in_specs=[VMEM],
        out_specs=VMEM,
        out_shape=in_vmem(parties, rows, width, dtype=bf16),
        compiler_params=params(),
        name="copies",
    )(state)
    return lax.cond(is_last, exchanged, lambda tiles: tiles, message)


def columns_first(state):
    return jnp.swapaxes(state, 1, 2).reshape(-1, state.shape[1])


def rows_first(state, share):
    return jnp.swapaxes(state.reshape(-1, share, state.shape[1]), 1, 2)


def body(
    queries, key_vectors, values, token_rates, fast_weights, momenta, fresh_weights, fresh_momenta
):
    sections, _, blocks, count, _ = queries.shape
    parties = lax.axis_size(TOK)
    share = fast_weights.shape[3]
    place_in_chain = lax.axis_index("seg")
    first = (place_in_chain == 0).astype(jnp.int32).reshape(1)
    is_last = place_in_chain == lax.axis_size("seg") - 1
    weights, moment = columns_first(fast_weights[0]), columns_first(momenta[0])
    fresh_weights, fresh_moment = columns_first(fresh_weights), columns_first(fresh_momenta)
    rows, shape = weights.shape[0], queries.shape
    places = [(section, 0, block) for section in range(sections) for block in range(blocks)]
    message, token = spread(weights, parties)
    *staged, _ = stage(token, places[0], (key_vectors, values))
    gathered = exchanged(message)
    results = squares = owed = None
    pending = []
    for index, place in enumerate(places):
        last = index == len(places) - 1
        leaving = not last and place[2] == blocks - 1
        if last:
            ahead = ((queries, place),)
        else:
            ahead = ((key_vectors, places[index + 1]), (values, places[index + 1]))
        message, *staged = grads(
            gathered, token_rates, *staged, (place[0], place[2]), ahead
        )
        arrived = exchanged(message)
        token = None
        if pending:
            results, token = apply_fast(*pending.pop(), results, shape)
        message, *state = update(index, arrived, weights, moment, squares, token, leaving)
        if leaving:
            own = gathered_by_last(is_last, message, rows, parties)
            weights, moment, message = enter(
                first, passed_on(message), fresh_weights, fresh_moment, parties
            )
            gathered = exchanged(message)
            owed = (handed_back(gathered), queries, place)
        else:
            weights, moment, squares = (*state, squares)[:3]
            gathered = exchanged(message)
            pending.append((gathered, queries, place))
    pending.pop()
    flag = is_last.astype(jnp.int32).reshape(1)
    results, token = apply_fast(*owed, results, shape, weights, instead=(own, flag))
    results, _ = apply_fast(gathered, staged[0], places[-1], results, shape, token, parts=2)
    return (results, rows_first(weights, share)[None], rows_first(moment, share)[None])


def solution(mesh):
    finer = Mesh(mesh.devices.reshape(mesh.shape["seg"], 4, 4), ("seg", "tok_0", "tok_1"))
    placed = (
        P(None, "seg", None, TOK, None),
        P(None, "seg", None, TOK, None),
        P(None, "seg", None, TOK, None),
        P(None, "seg", None, TOK),
        P("seg", None, None, TOK),
        P("seg", None, None, TOK),
        P(None, None, TOK),
        P(None, None, TOK),
    )
    return jax.shard_map(
        body,
        mesh=finer,
        in_specs=placed,
        out_specs=(
            P(None, "seg", None, TOK, None),
            P("seg", None, None, TOK),
            P("seg", None, None, TOK),
        ),
        check_vma=False,
    )
```

```python
import functools

import jax
import jax.numpy as jnp
from jax import lax
from jax.experimental import pallas as pl
from jax.experimental.pallas import tpu as pltpu
from jax.sharding import Mesh
from jax.sharding import PartitionSpec as P

TOK = ("tok_0", "tok_1")

momentum_decay = 0.9
learn_rate = 0.05
epsilon = 1e-06

f32, bf16 = jnp.float32, jnp.bfloat16
VMEM_LIMIT = 16 * 1024 * 1024

NN = (((1,), (0,)), ((), ()))
NT = (((1,), (1,)), ((), ()))


def dot(a, b, dims):
    return lax.dot_general(a, b, dims, preferred_element_type=f32)


def sigmoid(a):
    return 0.5 * jnp.tanh(0.5 * a) + 0.5


def matrix(gathered_ref, index, share):
    tiles = gathered_ref[:, index * share : (index + 1) * share, :]
    return tiles.reshape(-1, tiles.shape[-1])


def params(**more):
    return pltpu.CompilerParams(vmem_limit_bytes=VMEM_LIMIT, **more)


def in_vmem(*shape, dtype=f32):
    return pltpu.VMEM(shape, dtype)


VMEM = pl.BlockSpec(memory_space=pltpu.VMEM)
HBM = pl.BlockSpec(memory_space=pltpu.HBM)
SMEM = pl.BlockSpec(memory_space=pltpu.SMEM)


TOKEN = jax.ShapeDtypeStruct((8, 128), f32)


def in_hbm(array):
    return pltpu.with_memory_space_constraint(array, pltpu.HBM)


def started(sources, targets, places, sems):
    copies = [
        pltpu.make_async_copy(source.at[*place], target, sems.at[index])
        for index, (source, target, place) in enumerate(zip(sources, targets, places))
    ]
    for copy in copies:
        copy.start()
    return copies


def rows_in_vmem(array):
    return in_vmem(*array.shape[3:], dtype=array.dtype)


def spread_kernel(weights_ref, message_ref, token_ref, held_ref, sem):
    copy = pltpu.make_async_copy(weights_ref, held_ref, sem)
    copy.start()
    token_ref[...] = jnp.zeros_like(token_ref)
    copy.wait()
    message_ref[...] = jnp.broadcast_to(held_ref[...].astype(bf16)[None], message_ref.shape)


def spread(weights, parties):
    rows, width = weights.shape
    return pl.pallas_call(
        spread_kernel,
        in_specs=[HBM],
        out_specs=[VMEM] * 2,
        out_shape=[in_vmem(parties, rows, width, dtype=bf16), TOKEN],
        scratch_shapes=[pltpu.VMEM((rows, width), f32), pltpu.SemaphoreType.DMA],
        compiler_params=params(),
        name="spread",
    )(in_hbm(weights))


def copies_kernel(state_ref, message_ref):
    rows = message_ref.shape[1]
    message_ref[...] = jnp.broadcast_to(state_ref[:rows, :][None], message_ref.shape)


def stage_kernel(places, *refs):
    count = len(places)
    token_ref, sems = refs[-2:]
    copies = started(refs[1 : 1 + count], refs[-2 - count : -2], places, sems)
    token_ref[...] = jnp.zeros_like(token_ref)
    for copy in copies:
        copy.wait()


def stage(token, place, arrays):
    count = len(arrays)
    return pl.pallas_call(
        functools.partial(stage_kernel, [place] * count),
        in_specs=[VMEM] + [HBM] * count,
        out_specs=[VMEM] * (count + 1),
        out_shape=[rows_in_vmem(array) for array in arrays] + [TOKEN],
        scratch_shapes=[pltpu.SemaphoreType.DMA((count,))],
        compiler_params=params(),
        cost_estimate=pl.CostEstimate(
            flops=0, bytes_accessed=count * arrays[0].size, transcendentals=0
        ),
        name="stage",
    )(token, *(in_hbm(array) for array in arrays))


def grads_kernel(place, tile, ahead, gathered_ref, rate_ref, key_rows, value_rows, *refs):
    later = len(ahead)
    message_ref = refs[later]
    left_ref, back_ref, sems = refs[-3:]
    copies = started(refs[:later], refs[later + 1 : 2 * later + 1], ahead, sems)
    parties, rows, width = message_ref.shape
    share = width // parties
    count = key_rows.shape[0]
    section, block = place
    left_ref[...] = matrix(gathered_ref, 1, share).astype(f32).T.astype(bf16)
    gate, up = matrix(gathered_ref, 0, share), matrix(gathered_ref, 2, share)
    for start in range(0, count, tile):
        span = slice(start, start + tile)
        keys, values = key_rows[span, :], value_rows[span, :]
        rate = rate_ref[section, 0, block : block + 1, span]
        pre_gate = dot(gate, keys, NT)
        pre_up = dot(up, keys, NT)
        back = dot(left_ref[...], values, NT) * -rate
        sig = sigmoid(pre_gate)
        active = pre_gate * sig
        slope = sig + active * (1.0 - sig)
        back_ref[0, :, span] = (back * pre_up * slope).astype(bf16)
        back_ref[1, :, span] = (active * pre_up * rate).astype(bf16)
        back_ref[2, :, span] = (back * active).astype(bf16)
    keys, values = key_rows[...], value_rows[...]
    gradients = (
        dot(back_ref[0], keys, NN),
        -dot(back_ref[1], values, NN).T,
        dot(back_ref[2], keys, NN),
    )
    for index, gradient in enumerate(gradients):
        message_ref[:, index * share : (index + 1) * share, :] = gradient.astype(bf16).reshape(
            parties, share, width
        )
    if rows > 3 * share:
        row = lax.broadcasted_iota(jnp.int32, (share, width), 0)
        extra = jnp.zeros((share, width), f32)
        blocks = rate_ref.shape[2]
        for index in range(rate_ref.shape[0] * blocks):
            each = index % blocks
            rates = rate_ref[index // blocks, 0, each : each + 1, :]
            square = jnp.sum(rates * rates, axis=1, keepdims=True)
            high = square.astype(bf16).astype(f32)
            extra = jnp.where(row == 2 * index, high, extra)
            extra = jnp.where(row == 2 * index + 1, square - high, extra)
        message_ref[:, 3 * share :, :] = jnp.broadcast_to(
            extra.astype(bf16)[None], (parties, share, width)
        )
    for copy in copies:
        copy.wait()


def grads(gathered, rates, keys, values, place, ahead):
    parties, _, width = gathered.shape
    share = width // parties
    count = keys.shape[0]
    rows = (4 if place == (0, 0) else 3) * share
    return pl.pallas_call(
        functools.partial(grads_kernel, place, 256, [where for _, where in ahead]),
        in_specs=[VMEM] * 4 + [HBM] * len(ahead),
        out_specs=[VMEM] * (1 + len(ahead)),
        out_shape=[in_vmem(parties, rows, width, dtype=bf16)]
        + [rows_in_vmem(array) for array, _ in ahead],
        scratch_shapes=[
            pltpu.VMEM((width, width), bf16),
            pltpu.VMEM((3, width, count), bf16),
            pltpu.SemaphoreType.DMA((len(ahead),)),
        ],
        compiler_params=params(),
        cost_estimate=pl.CostEstimate(
            flops=12 * count * width * width, bytes_accessed=4 * count * width, transcendentals=0
        ),
        name="grads",
    )(gathered, rates, keys, values, *(in_hbm(array) for array, _ in ahead))


def update_kernel(index, waits, *refs):
    arrived_ref, weights_ref, moment_ref = refs[:3]
    refs = refs[3:]
    rows = weights_ref.shape[0]
    gradients = jnp.sum(arrived_ref[:, :rows, :].astype(f32), axis=0)
    if index == 0:
        squares = jnp.sum(arrived_ref[:, rows:, :].astype(f32), axis=0)
        refs[-1][...] = squares
    else:
        squares, refs = refs[0][...], refs[1:]
    square = squares[2 * index : 2 * index + 1, :] + squares[2 * index + 1 : 2 * index + 2, :]
    weights = weights_ref[...]
    moment = momentum_decay * moment_ref[...] + gradients * lax.rsqrt(square)
    stepped = weights - learn_rate * moment
    rescale = jnp.sqrt(
        jnp.sum(weights * weights, axis=1, keepdims=True)
        / (jnp.sum(stepped * stepped, axis=1, keepdims=True) + epsilon)
    )
    weights = stepped * rescale
    rounded = weights.astype(bf16)
    refs = refs[waits:]
    message_ref = refs[0]
    if len(message_ref.shape) == 3:
        message_ref[...] = jnp.broadcast_to(rounded[None], message_ref.shape)
        refs[1][...] = weights
        refs[2][...] = moment
    else:
        message_ref[:rows, :] = rounded
        message_ref[rows:, :] = moment.astype(bf16)


def update(index, arrived, weights, moment, squares, token, leaving):
    rows, width = weights.shape
    given, in_specs = [arrived, weights, moment], [VMEM] * 3
    if index > 0:
        given.append(squares)
        in_specs.append(VMEM)
    waits = token is not None
    if waits:
        given.append(token)
        in_specs.append(VMEM)
    if leaving:
        out_shape = [in_vmem(2 * rows, width, dtype=bf16)]
    else:
        out_shape = [in_vmem(arrived.shape[0], rows, width, dtype=bf16)]
        out_shape += [in_vmem(rows, width)] * 2
    if index == 0:
        out_shape.append(in_vmem(arrived.shape[1] - rows, width))
    return pl.pallas_call(
        functools.partial(update_kernel, index, waits),
        in_specs=in_specs,
        out_specs=[VMEM] * len(out_shape),
        out_shape=out_shape,
        compiler_params=params(),
        name="update",
    )(*given)


def enter_kernel(
    first_ref,
    passed_ref,
    fresh_weights_ref,
    fresh_moment_ref,
    wait_ref,
    weights_ref,
    moment_ref,
    message_ref,
):
    rows = weights_ref.shape[0]
    first = first_ref[0] == 1
    passed = passed_ref[...].astype(f32)
    weights = jnp.where(first, fresh_weights_ref[...], passed[:rows])
    weights_ref[...] = weights
    moment_ref[...] = jnp.where(first, fresh_moment_ref[...], passed[rows:])
    message_ref[...] = jnp.broadcast_to(weights.astype(bf16)[None], message_ref.shape)


def enter(first, passed, fresh_weights, fresh_moment, token, parties):
    rows, width = fresh_weights.shape
    return pl.pallas_call(
        enter_kernel,
        in_specs=[SMEM] + [VMEM] * 4,
        out_specs=[VMEM] * 3,
        out_shape=[
            in_vmem(rows, width),
            in_vmem(rows, width),
            in_vmem(parties, rows, width, dtype=bf16),
        ],
        compiler_params=params(),
        name="enter",
    )(first, passed, fresh_weights, fresh_moment, token)


def apply_kernel(place, staged, waits, chosen, parts, gathered_ref, query_ref, *refs):
    refs = refs[waits:]
    if chosen:
        gathered_ref = jnp.where(refs[1][0] == 1, refs[0][...], gathered_ref[...])
    out_ref, token_ref, query_rows, held_ref, sems = refs[-5:]
    token_ref[...] = jnp.zeros_like(token_ref)
    length, width = query_rows.shape
    share = width // gathered_ref.shape[0]
    if staged:
        query_rows = query_ref
    else:
        (copy,) = started([query_ref], [query_rows], [place], sems)
        copy.wait()
    size = length // parts
    copies = []
    for part in range(parts):
        queries = query_rows[part * size : (part + 1) * size, :]
        pre_gate = dot(queries, matrix(gathered_ref, 0, share), NT)
        pre_up = dot(queries, matrix(gathered_ref, 2, share), NT)
        hidden = (pre_gate * sigmoid(pre_gate) * pre_up).astype(bf16)
        held_ref[part * size : (part + 1) * size, :] = dot(
            hidden, matrix(gathered_ref, 1, share), NT
        ).astype(bf16)
        span = pl.ds(part * size, size)
        copies.append(
            pltpu.make_async_copy(
                held_ref.at[span, :], out_ref.at[*place].at[span, :], sems.at[1 + part]
            )
        )
        copies[-1].start()
    for copy in copies:
        copy.wait()


def apply_fast(gathered, queries, place, results, shape, token=None, parts=1, instead=()):
    count, width = shape[3:]
    staged = len(queries.shape) == 2
    waits = token is not None
    given = [gathered, queries if staged else in_hbm(queries)]
    in_specs = [VMEM, VMEM if staged else HBM]
    if waits:
        given.append(token)
        in_specs.append(VMEM)
    if instead:
        given += instead
        in_specs += [VMEM, SMEM]
    if results is not None:
        given.append(results)
        in_specs.append(HBM)
    return pl.pallas_call(
        functools.partial(apply_kernel, place, staged, waits, bool(instead), parts),
        in_specs=in_specs,
        out_specs=[HBM, VMEM],
        out_shape=[jax.ShapeDtypeStruct(shape, bf16), TOKEN],
        input_output_aliases={} if results is None else {len(given) - 1: 0},
        scratch_shapes=[
            pltpu.VMEM((count, width), bf16),
            pltpu.VMEM((count, width), bf16),
            pltpu.SemaphoreType.DMA((1 + parts,)),
        ],
        compiler_params=params(),
        cost_estimate=pl.CostEstimate(
            flops=6 * count * width * width, bytes_accessed=4 * count * width, transcendentals=0
        ),
        name="apply",
    )(*given)


def exchanged(tiles):
    return lax.all_to_all(tiles, TOK, split_axis=0, concat_axis=0, tiled=True)


def passed_on(array):
    length = lax.axis_size("seg")
    return lax.ppermute(array, "seg", [(i, i + 1) for i in range(length - 1)])


def handed_back(array):
    length = lax.axis_size("seg")
    return lax.ppermute(array, "seg", [(i + 1, i) for i in range(length - 1)])


def gathered_by_last(is_last, state, rows, parties):
    width = state.shape[1]
    message = pl.pallas_call(
        copies_kernel,
        in_specs=[VMEM],
        out_specs=VMEM,
        out_shape=in_vmem(parties, rows, width, dtype=bf16),
        compiler_params=params(),
        name="copies",
    )(state)
    return lax.cond(is_last, exchanged, lambda tiles: tiles, message)


def columns_first(state):
    return jnp.swapaxes(state, 1, 2).reshape(-1, state.shape[1])


def rows_first(state, share):
    return jnp.swapaxes(state.reshape(-1, share, state.shape[1]), 1, 2)


def body(
    queries, key_vectors, values, token_rates, fast_weights, momenta, fresh_weights, fresh_momenta
):
    sections, _, blocks, count, _ = queries.shape
    parties = lax.axis_size(TOK)
    share = fast_weights.shape[3]
    place_in_chain = lax.axis_index("seg")
    first = (place_in_chain == 0).astype(jnp.int32).reshape(1)
    is_last = place_in_chain == lax.axis_size("seg") - 1
    weights, moment = columns_first(fast_weights[0]), columns_first(momenta[0])
    fresh_weights, fresh_moment = columns_first(fresh_weights), columns_first(fresh_momenta)
    rows, shape = weights.shape[0], queries.shape
    places = [(section, 0, block) for section in range(sections) for block in range(blocks)]
    message, token = spread(weights, parties)
    *staged, _ = stage(token, places[0], (key_vectors, values))
    gathered = exchanged(message)
    results = squares = owed = None
    pending = []
    for index, place in enumerate(places):
        last = index == len(places) - 1
        leaving = not last and place[2] == blocks - 1
        if last:
            ahead = ((queries, place),)
        else:
            ahead = ((key_vectors, places[index + 1]), (values, places[index + 1]))
        message, *staged = grads(
            gathered, token_rates, *staged, (place[0], place[2]), ahead
        )
        arrived = exchanged(message)
        token = None
        if pending and not leaving:
            results, token = apply_fast(*pending.pop(), results, shape)
        message, *state = update(index, arrived, weights, moment, squares, token, leaving)
        if leaving:
            passed = passed_on(message)
            results, token = apply_fast(*pending.pop(), results, shape, message)
            own = gathered_by_last(is_last, message, rows, parties)
            weights, moment, message = enter(
                first, passed, fresh_weights, fresh_moment, token, parties
            )
            gathered = exchanged(message)
            owed = (handed_back(gathered), queries, place)
        else:
            weights, moment, squares = (*state, squares)[:3]
            gathered = exchanged(message)
            pending.append((gathered, queries, place))
    pending.pop()
    flag = is_last.astype(jnp.int32).reshape(1)
    results, token = apply_fast(*owed, results, shape, weights, instead=(own, flag))
    results, _ = apply_fast(gathered, staged[0], places[-1], results, shape, token, parts=2)
    return (results, rows_first(weights, share)[None], rows_first(moment, share)[None])


def solution(mesh):
    finer = Mesh(mesh.devices.reshape(mesh.shape["seg"], 4, 4), ("seg", "tok_0", "tok_1"))
    placed = (
        P(None, "seg", None, TOK, None),
        P(None, "seg", None, TOK, None),
        P(None, "seg", None, TOK, None),
        P(None, "seg", None, TOK),
        P("seg", None, None, TOK),
        P("seg", None, None, TOK),
        P(None, None, TOK),
        P(None, None, TOK),
    )
    return jax.shard_map(
        body,
        mesh=finer,
        in_specs=placed,
        out_specs=(
            P(None, "seg", None, TOK, None),
            P("seg", None, None, TOK),
            P("seg", None, None, TOK),
        ),
        check_vma=False,
    )
```

```python
import functools

import jax
import jax.numpy as jnp
from jax import lax
from jax.experimental import pallas as pl
from jax.experimental.pallas import tpu as pltpu
from jax.sharding import Mesh
from jax.sharding import PartitionSpec as P

TOK = ("tok_0", "tok_1")

momentum_decay = 0.9
learn_rate = 0.05
epsilon = 1e-06

f32, bf16 = jnp.float32, jnp.bfloat16
VMEM_LIMIT = 16 * 1024 * 1024

NN = (((1,), (0,)), ((), ()))
NT = (((1,), (1,)), ((), ()))


def dot(a, b, dims):
    return lax.dot_general(a, b, dims, preferred_element_type=f32)


def sigmoid(a):
    return 0.5 * jnp.tanh(0.5 * a) + 0.5


def matrix(gathered_ref, index, share):
    tiles = gathered_ref[:, index * share : (index + 1) * share, :]
    return tiles.reshape(-1, tiles.shape[-1])


def params(**more):
    return pltpu.CompilerParams(vmem_limit_bytes=VMEM_LIMIT, **more)


def in_vmem(*shape, dtype=f32):
    return pltpu.VMEM(shape, dtype)


VMEM = pl.BlockSpec(memory_space=pltpu.VMEM)
HBM = pl.BlockSpec(memory_space=pltpu.HBM)
SMEM = pl.BlockSpec(memory_space=pltpu.SMEM)


TOKEN = jax.ShapeDtypeStruct((8, 128), f32)


def in_hbm(array):
    return pltpu.with_memory_space_constraint(array, pltpu.HBM)


def started(sources, targets, places, sems):
    copies = [
        pltpu.make_async_copy(source.at[*place], target, sems.at[index])
        for index, (source, target, place) in enumerate(zip(sources, targets, places))
    ]
    for copy in copies:
        copy.start()
    return copies


def rows_in_vmem(array):
    return in_vmem(*array.shape[3:], dtype=array.dtype)


def spread_kernel(weights_ref, message_ref, token_ref, held_ref, sem):
    copy = pltpu.make_async_copy(weights_ref, held_ref, sem)
    copy.start()
    token_ref[...] = jnp.zeros_like(token_ref)
    copy.wait()
    message_ref[...] = jnp.broadcast_to(held_ref[...].astype(bf16)[None], message_ref.shape)


def spread(weights, parties):
    rows, width = weights.shape
    return pl.pallas_call(
        spread_kernel,
        in_specs=[HBM],
        out_specs=[VMEM] * 2,
        out_shape=[in_vmem(parties, rows, width, dtype=bf16), TOKEN],
        scratch_shapes=[pltpu.VMEM((rows, width), f32), pltpu.SemaphoreType.DMA],
        compiler_params=params(),
        name="spread",
    )(in_hbm(weights))


def copies_kernel(state_ref, message_ref):
    rows = message_ref.shape[1]
    message_ref[...] = jnp.broadcast_to(state_ref[:rows, :][None], message_ref.shape)


def stage_kernel(places, *refs):
    count = len(places)
    token_ref, sems = refs[-2:]
    copies = started(refs[2 : 2 + count], refs[-2 - count : -2], places, sems)
    token_ref[...] = jnp.zeros_like(token_ref)
    for copy in copies:
        copy.wait()


def stage(token, who, place, arrays):
    count = len(arrays)
    return pl.pallas_call(
        functools.partial(stage_kernel, [place] * count),
        in_specs=[VMEM, SMEM] + [HBM] * count,
        out_specs=[VMEM] * (count + 1),
        out_shape=[rows_in_vmem(array) for array in arrays] + [TOKEN],
        scratch_shapes=[pltpu.SemaphoreType.DMA((count,))],
        compiler_params=params(),
        cost_estimate=pl.CostEstimate(
            flops=0, bytes_accessed=count * arrays[0].size, transcendentals=0
        ),
        name="stage",
    )(token, who, *(in_hbm(array) for array in arrays))


def grads_kernel(place, tile, ahead, gathered_ref, rate_ref, key_rows, value_rows, *refs):
    later = len(ahead)
    message_ref = refs[later]
    left_ref, back_ref, sems = refs[-3:]
    copies = started(refs[:later], refs[later + 1 : 2 * later + 1], ahead, sems)
    parties, rows, width = message_ref.shape
    share = width // parties
    count = key_rows.shape[0]
    section, block = place
    left_ref[...] = matrix(gathered_ref, 1, share).astype(f32).T.astype(bf16)
    gate, up = matrix(gathered_ref, 0, share), matrix(gathered_ref, 2, share)
    for start in range(0, count, tile):
        span = slice(start, start + tile)
        keys, values = key_rows[span, :], value_rows[span, :]
        rate = rate_ref[section, 0, block : block + 1, span]
        pre_gate = dot(gate, keys, NT)
        pre_up = dot(up, keys, NT)
        back = dot(left_ref[...], values, NT) * -rate
        sig = sigmoid(pre_gate)
        active = pre_gate * sig
        slope = sig + active * (1.0 - sig)
        back_ref[0, :, span] = (back * pre_up * slope).astype(bf16)
        back_ref[1, :, span] = (active * pre_up * rate).astype(bf16)
        back_ref[2, :, span] = (back * active).astype(bf16)
    keys, values = key_rows[...], value_rows[...]
    gradients = (
        dot(back_ref[0], keys, NN),
        -dot(back_ref[1], values, NN).T,
        dot(back_ref[2], keys, NN),
    )
    for index, gradient in enumerate(gradients):
        message_ref[:, index * share : (index + 1) * share, :] = gradient.astype(bf16).reshape(
            parties, share, width
        )
    if rows > 3 * share:
        row = lax.broadcasted_iota(jnp.int32, (share, width), 0)
        extra = jnp.zeros((share, width), f32)
        blocks = rate_ref.shape[2]
        for index in range(rate_ref.shape[0] * blocks):
            each = index % blocks
            rates = rate_ref[index // blocks, 0, each : each + 1, :]
            square = jnp.sum(rates * rates, axis=1, keepdims=True)
            high = square.astype(bf16).astype(f32)
            extra = jnp.where(row == 2 * index, high, extra)
            extra = jnp.where(row == 2 * index + 1, square - high, extra)
        message_ref[:, 3 * share :, :] = jnp.broadcast_to(
            extra.astype(bf16)[None], (parties, share, width)
        )
    for copy in copies:
        copy.wait()


def grads(gathered, rates, keys, values, place, ahead):
    parties, _, width = gathered.shape
    share = width // parties
    count = keys.shape[0]
    rows = (4 if place == (0, 0) else 3) * share
    return pl.pallas_call(
        functools.partial(grads_kernel, place, 256, [where for _, where in ahead]),
        in_specs=[VMEM] * 4 + [HBM] * len(ahead),
        out_specs=[VMEM] * (1 + len(ahead)),
        out_shape=[in_vmem(parties, rows, width, dtype=bf16)]
        + [rows_in_vmem(array) for array, _ in ahead],
        scratch_shapes=[
            pltpu.VMEM((width, width), bf16),
            pltpu.VMEM((3, width, count), bf16),
            pltpu.SemaphoreType.DMA((len(ahead),)),
        ],
        compiler_params=params(),
        cost_estimate=pl.CostEstimate(
            flops=12 * count * width * width, bytes_accessed=4 * count * width, transcendentals=0
        ),
        name="grads",
    )(gathered, rates, keys, values, *(in_hbm(array) for array, _ in ahead))


def update_kernel(index, waits, *refs):
    arrived_ref, weights_ref, moment_ref = refs[:3]
    refs = refs[3:]
    rows = weights_ref.shape[0]
    gradients = jnp.sum(arrived_ref[:, :rows, :].astype(f32), axis=0)
    if index == 0:
        squares = jnp.sum(arrived_ref[:, rows:, :].astype(f32), axis=0)
        refs[-1][...] = squares
    else:
        squares, refs = refs[0][...], refs[1:]
    square = squares[2 * index : 2 * index + 1, :] + squares[2 * index + 1 : 2 * index + 2, :]
    weights = weights_ref[...]
    moment = momentum_decay * moment_ref[...] + gradients * lax.rsqrt(square)
    stepped = weights - learn_rate * moment
    rescale = jnp.sqrt(
        jnp.sum(weights * weights, axis=1, keepdims=True)
        / (jnp.sum(stepped * stepped, axis=1, keepdims=True) + epsilon)
    )
    weights = stepped * rescale
    rounded = weights.astype(bf16)
    refs = refs[waits:]
    message_ref = refs[0]
    if len(message_ref.shape) == 3:
        message_ref[...] = jnp.broadcast_to(rounded[None], message_ref.shape)
        refs[1][...] = weights
        refs[2][...] = moment
    else:
        message_ref[:rows, :] = rounded
        message_ref[rows:, :] = moment.astype(bf16)


def update(index, arrived, weights, moment, squares, token, leaving):
    rows, width = weights.shape
    given, in_specs = [arrived, weights, moment], [VMEM] * 3
    if index > 0:
        given.append(squares)
        in_specs.append(VMEM)
    waits = token is not None
    if waits:
        given.append(token)
        in_specs.append(VMEM)
    if leaving:
        out_shape = [in_vmem(2 * rows, width, dtype=bf16)]
    else:
        out_shape = [in_vmem(arrived.shape[0], rows, width, dtype=bf16)]
        out_shape += [in_vmem(rows, width)] * 2
    if index == 0:
        out_shape.append(in_vmem(arrived.shape[1] - rows, width))
    return pl.pallas_call(
        functools.partial(update_kernel, index, waits),
        in_specs=in_specs,
        out_specs=[VMEM] * len(out_shape),
        out_shape=out_shape,
        compiler_params=params(),
        name="update",
    )(*given)


def enter_kernel(
    first_ref,
    passed_ref,
    fresh_weights_ref,
    fresh_moment_ref,
    wait_ref,
    weights_ref,
    moment_ref,
    message_ref,
):
    rows = weights_ref.shape[0]
    first = first_ref[0] == 0
    passed = passed_ref[...].astype(f32)
    weights = jnp.where(first, fresh_weights_ref[...], passed[:rows])
    weights_ref[...] = weights
    moment_ref[...] = jnp.where(first, fresh_moment_ref[...], passed[rows:])
    message_ref[...] = jnp.broadcast_to(weights.astype(bf16)[None], message_ref.shape)


def enter(first, passed, fresh_weights, fresh_moment, token, parties):
    rows, width = fresh_weights.shape
    return pl.pallas_call(
        enter_kernel,
        in_specs=[SMEM] + [VMEM] * 4,
        out_specs=[VMEM] * 3,
        out_shape=[
            in_vmem(rows, width),
            in_vmem(rows, width),
            in_vmem(parties, rows, width, dtype=bf16),
        ],
        compiler_params=params(),
        name="enter",
    )(first, passed, fresh_weights, fresh_moment, token)


def apply_rows(place, parts, gathered, query_ref, query_rows, out_ref, held_ref, sems):
    length, width = query_rows.shape
    share = width // gathered.shape[0]
    if query_ref is not query_rows:
        (copy,) = started([query_ref], [query_rows], [place], sems)
        copy.wait()
    size = length // parts
    copies = []
    for part in range(parts):
        queries = query_rows[part * size : (part + 1) * size, :]
        pre_gate = dot(queries, matrix(gathered, 0, share), NT)
        pre_up = dot(queries, matrix(gathered, 2, share), NT)
        hidden = (pre_gate * sigmoid(pre_gate) * pre_up).astype(bf16)
        held_ref[part * size : (part + 1) * size, :] = dot(
            hidden, matrix(gathered, 1, share), NT
        ).astype(bf16)
        span = pl.ds(part * size, size)
        copies.append(
            pltpu.make_async_copy(
                held_ref.at[span, :], out_ref.at[*place].at[span, :], sems.at[1 + part]
            )
        )
        copies[-1].start()
    for copy in copies:
        copy.wait()


def apply_kernel(place, staged, waits, extra, when, aliased, hands, parts, gathered_ref, query_ref, *refs):
    wait_ref, refs = (refs[0], refs[1:]) if waits else (None, refs)
    extra_refs, refs = refs[: len(extra)], refs[len(extra) + aliased :]
    out_ref, query_rows, held_ref, sems = refs[0], *refs[-3:]
    if hands:
        refs[1][...] = wait_ref[...] if waits else jnp.zeros_like(refs[1])
    rows_ref = query_ref if staged else query_rows
    if extra == ("instead", "who"):
        gathered_ref = jnp.where(when(extra_refs[1][0]), extra_refs[0][...], gathered_ref[...])
    if extra == ("who",):

        @pl.when(when(extra_refs[0][0]))
        def _():
            apply_rows(place, parts, gathered_ref, query_ref, rows_ref, out_ref, held_ref, sems)

    else:
        apply_rows(place, parts, gathered_ref, query_ref, rows_ref, out_ref, held_ref, sems)


def apply_fast(
    gathered, queries, place, results, shape, token=None, parts=1, instead=None, who=None, when=None, hands=True
):
    count, width = shape[3:]
    staged = len(queries.shape) == 2
    waits = token is not None
    given = [gathered, queries if staged else in_hbm(queries)]
    in_specs = [VMEM, VMEM if staged else HBM]
    extra = ()
    if waits:
        given.append(token)
        in_specs.append(VMEM)
    if instead is not None:
        given.append(instead)
        in_specs.append(VMEM)
        extra += ("instead",)
    if who is not None:
        given.append(who)
        in_specs.append(SMEM)
        extra += ("who",)
    if results is not None:
        given.append(results)
        in_specs.append(HBM)
    out_shape = [jax.ShapeDtypeStruct(shape, bf16)]
    if hands:
        out_shape.append(in_vmem(*token.shape, dtype=token.dtype) if waits else TOKEN)
    results, *handed = pl.pallas_call(
        functools.partial(
            apply_kernel, place, staged, waits, extra, when, int(results is not None), hands, parts
        ),
        in_specs=in_specs,
        out_specs=[HBM] + [VMEM] * hands,
        out_shape=out_shape,
        input_output_aliases={} if results is None else {len(given) - 1: 0},
        scratch_shapes=[
            pltpu.VMEM((count, width), bf16),
            pltpu.VMEM((count, width), bf16),
            pltpu.SemaphoreType.DMA((1 + parts,)),
        ],
        compiler_params=params(),
        cost_estimate=pl.CostEstimate(
            flops=6 * count * width * width, bytes_accessed=4 * count * width, transcendentals=0
        ),
        name="apply",
    )(*given)
    return (results, *handed)


def exchanged(tiles):
    return lax.all_to_all(tiles, TOK, split_axis=0, concat_axis=0, tiled=True)


def passed_on(array):
    length = lax.axis_size("seg")
    return lax.ppermute(array, "seg", [(i, i + 1) for i in range(length - 1)])


def handed_back(array):
    length = lax.axis_size("seg")
    return lax.ppermute(array, "seg", [(i + 1, i) for i in range(length - 1)])


def gathered_by_last(is_last, state, rows, parties):
    width = state.shape[1]
    message = pl.pallas_call(
        copies_kernel,
        in_specs=[VMEM],
        out_specs=VMEM,
        out_shape=in_vmem(parties, rows, width, dtype=bf16),
        compiler_params=params(),
        name="copies",
    )(state)
    return lax.cond(is_last, exchanged, lambda tiles: tiles, message)


def columns_first(state):
    return jnp.swapaxes(state, 1, 2).reshape(-1, state.shape[1])


def rows_first(state, share):
    return jnp.swapaxes(state.reshape(-1, share, state.shape[1]), 1, 2)


def body(
    queries, key_vectors, values, token_rates, fast_weights, momenta, fresh_weights, fresh_momenta
):
    sections, _, blocks, count, _ = queries.shape
    parties = lax.axis_size(TOK)
    share = fast_weights.shape[3]
    place_in_chain = lax.axis_index("seg")
    who = place_in_chain.reshape(1)
    length = lax.axis_size("seg")
    is_last = place_in_chain == length - 1

    def early(segment):
        return (segment % 2 == 1) & (segment != length - 1)

    def late(segment):
        return (segment % 2 == 0) | (segment == length - 1)

    def at_end(segment):
        return segment == length - 1

    weights, moment = columns_first(fast_weights[0]), columns_first(momenta[0])
    fresh_weights, fresh_moment = columns_first(fresh_weights), columns_first(fresh_momenta)
    rows, shape = weights.shape[0], queries.shape
    places = [(section, 0, block) for section in range(sections) for block in range(blocks)]
    message, token = spread(weights, parties)
    *staged, _ = stage(token, who, places[0], (key_vectors, values))
    gathered = exchanged(message)
    results = squares = owed = None
    pending = []
    for index, place in enumerate(places):
        last = index == len(places) - 1
        leaving = not last and place[2] == blocks - 1
        if last:
            ahead = ((queries, place),)
        else:
            ahead = ((key_vectors, places[index + 1]), (values, places[index + 1]))
        message, *staged = grads(
            gathered, token_rates, *staged, (place[0], place[2]), ahead
        )
        arrived = exchanged(message)
        token = None
        if pending and not leaving:
            results, token = apply_fast(*pending.pop(), results, shape)
        message, *state = update(index, arrived, weights, moment, squares, token, leaving)
        if leaving:
            here = pending.pop()
            results, message = apply_fast(*here, results, shape, message, who=who, when=early)
            passed = passed_on(message)
            results, token = apply_fast(*here, results, shape, message, who=who, when=late)
            own = gathered_by_last(is_last, message, rows, parties)
            weights, moment, message = enter(
                who, passed, fresh_weights, fresh_moment, token, parties
            )
            gathered = exchanged(message)
            owed = (handed_back(gathered), queries, place)
        else:
            weights, moment, squares = (*state, squares)[:3]
            gathered = exchanged(message)
            pending.append((gathered, queries, place))
    pending.pop()
    results, token = apply_fast(*owed, results, shape, weights, instead=own, who=who, when=at_end)
    (results,) = apply_fast(
        gathered, staged[0], places[-1], results, shape, token, parts=2, hands=False
    )
    return (results, rows_first(weights, share)[None], rows_first(moment, share)[None])


def solution(mesh):
    finer = Mesh(mesh.devices.reshape(mesh.shape["seg"], 4, 4), ("seg", "tok_0", "tok_1"))
    placed = (
        P(None, "seg", None, TOK, None),
        P(None, "seg", None, TOK, None),
        P(None, "seg", None, TOK, None),
        P(None, "seg", None, TOK),
        P("seg", None, None, TOK),
        P("seg", None, None, TOK),
        P(None, None, TOK),
        P(None, None, TOK),
    )
    return jax.shard_map(
        body,
        mesh=finer,
        in_specs=placed,
        out_specs=(
            P(None, "seg", None, TOK, None),
            P("seg", None, None, TOK),
            P("seg", None, None, TOK),
        ),
        check_vma=False,
    )
```

```python
import functools

import jax
import jax.numpy as jnp
from jax import lax
from jax.experimental import pallas as pl
from jax.experimental.pallas import tpu as pltpu
from jax.sharding import Mesh
from jax.sharding import PartitionSpec as P

TOK = ("tok_0", "tok_1")

momentum_decay = 0.9
learn_rate = 0.05
epsilon = 1e-06

f32, bf16 = jnp.float32, jnp.bfloat16
VMEM_LIMIT = 16 * 1024 * 1024

NN = (((1,), (0,)), ((), ()))
NT = (((1,), (1,)), ((), ()))


def dot(a, b, dims):
    return lax.dot_general(a, b, dims, preferred_element_type=f32)


def sigmoid(a):
    return 0.5 * jnp.tanh(0.5 * a) + 0.5


def matrix(gathered_ref, index, share):
    tiles = gathered_ref[:, index * share : (index + 1) * share, :]
    return tiles.reshape(-1, tiles.shape[-1])


def params(**more):
    return pltpu.CompilerParams(vmem_limit_bytes=VMEM_LIMIT, **more)


def in_vmem(*shape, dtype=f32):
    return pltpu.VMEM(shape, dtype)


VMEM = pl.BlockSpec(memory_space=pltpu.VMEM)
HBM = pl.BlockSpec(memory_space=pltpu.HBM)
SMEM = pl.BlockSpec(memory_space=pltpu.SMEM)


TOKEN = jax.ShapeDtypeStruct((8, 128), f32)


def in_hbm(array):
    return pltpu.with_memory_space_constraint(array, pltpu.HBM)


def started(sources, targets, places, sems):
    copies = [
        pltpu.make_async_copy(source.at[*place], target, sems.at[index])
        for index, (source, target, place) in enumerate(zip(sources, targets, places))
    ]
    for copy in copies:
        copy.start()
    return copies


def rows_in_vmem(array):
    return in_vmem(*array.shape[3:], dtype=array.dtype)


def spread_kernel(weights_ref, message_ref, token_ref, held_ref, sem):
    copy = pltpu.make_async_copy(weights_ref, held_ref, sem)
    copy.start()
    token_ref[...] = jnp.zeros_like(token_ref)
    copy.wait()
    message_ref[...] = jnp.broadcast_to(held_ref[...].astype(bf16)[None], message_ref.shape)


def spread(weights, parties):
    rows, width = weights.shape
    return pl.pallas_call(
        spread_kernel,
        in_specs=[HBM],
        out_specs=[VMEM] * 2,
        out_shape=[in_vmem(parties, rows, width, dtype=bf16), TOKEN],
        scratch_shapes=[pltpu.VMEM((rows, width), f32), pltpu.SemaphoreType.DMA],
        compiler_params=params(),
        name="spread",
    )(in_hbm(weights))


def copies_kernel(state_ref, message_ref):
    rows = message_ref.shape[1]
    message_ref[...] = jnp.broadcast_to(state_ref[:rows, :][None], message_ref.shape)


def stage_kernel(places, *refs):
    count = len(places)
    token_ref, sems = refs[-2:]
    copies = started(refs[2 : 2 + count], refs[-2 - count : -2], places, sems)
    token_ref[...] = jnp.zeros_like(token_ref)
    for copy in copies:
        copy.wait()


def stage(token, who, place, arrays):
    count = len(arrays)
    return pl.pallas_call(
        functools.partial(stage_kernel, [place] * count),
        in_specs=[VMEM, SMEM] + [HBM] * count,
        out_specs=[VMEM] * (count + 1),
        out_shape=[rows_in_vmem(array) for array in arrays] + [TOKEN],
        scratch_shapes=[pltpu.SemaphoreType.DMA((count,))],
        compiler_params=params(),
        cost_estimate=pl.CostEstimate(
            flops=0, bytes_accessed=count * arrays[0].size, transcendentals=0
        ),
        name="stage",
    )(token, who, *(in_hbm(array) for array in arrays))


def grads_kernel(place, tile, ahead, gathered_ref, rate_ref, key_rows, value_rows, *refs):
    later = len(ahead)
    message_ref = refs[later]
    left_ref, back_ref, sems = refs[-3:]
    copies = started(refs[:later], refs[later + 1 : 2 * later + 1], ahead, sems)
    parties, rows, lanes = message_ref.shape
    width = gathered_ref.shape[2]
    share = width // parties
    count = key_rows.shape[0]
    section, block = place
    left_ref[...] = matrix(gathered_ref, 1, share).astype(f32).T.astype(bf16)
    gate, up = matrix(gathered_ref, 0, share), matrix(gathered_ref, 2, share)
    for start in range(0, count, tile):
        span = slice(start, start + tile)
        keys, values = key_rows[span, :], value_rows[span, :]
        rate = rate_ref[section, 0, block : block + 1, span]
        pre_gate = dot(gate, keys, NT)
        pre_up = dot(up, keys, NT)
        back = dot(left_ref[...], values, NT) * -rate
        sig = sigmoid(pre_gate)
        active = pre_gate * sig
        slope = sig + active * (1.0 - sig)
        back_ref[0, :, span] = (back * pre_up * slope).astype(bf16)
        back_ref[1, :, span] = (active * pre_up * rate).astype(bf16)
        back_ref[2, :, span] = (back * active).astype(bf16)
    keys, values = key_rows[...], value_rows[...]
    gradients = (
        dot(back_ref[0], keys, NN),
        -dot(back_ref[1], values, NN).T,
        dot(back_ref[2], keys, NN),
    )
    for index, gradient in enumerate(gradients):
        tiles = gradient.astype(bf16).reshape(parties, share, width)
        for half in range(width // lanes):
            start = (3 * half + index) * share
            message_ref[:, start : start + share, :] = tiles[
                :, :, half * lanes : (half + 1) * lanes
            ]
    used = 3 * share * (width // lanes)
    if rows > used:
        row = lax.broadcasted_iota(jnp.int32, (share, lanes), 0)
        extra = jnp.zeros((share, lanes), f32)
        blocks = rate_ref.shape[2]
        for index in range(rate_ref.shape[0] * blocks):
            each = index % blocks
            rates = rate_ref[index // blocks, 0, each : each + 1, :]
            square = jnp.sum(rates * rates, axis=1, keepdims=True)
            high = square.astype(bf16).astype(f32)
            extra = jnp.where(row == 2 * index, high, extra)
            extra = jnp.where(row == 2 * index + 1, square - high, extra)
        message_ref[:, used:, :] = jnp.broadcast_to(
            extra.astype(bf16)[None], (parties, share, lanes)
        )
    for copy in copies:
        copy.wait()


def grads(gathered, rates, keys, values, place, ahead):
    parties, _, width = gathered.shape
    share = width // parties
    count = keys.shape[0]
    if place == (0, 0):
        lanes = width // 2
        rows = 7 * share
    else:
        lanes = width
        rows = 3 * share
    return pl.pallas_call(
        functools.partial(grads_kernel, place, 256, [where for _, where in ahead]),
        in_specs=[VMEM] * 4 + [HBM] * len(ahead),
        out_specs=[VMEM] * (1 + len(ahead)),
        out_shape=[in_vmem(parties, rows, lanes, dtype=bf16)]
        + [rows_in_vmem(array) for array, _ in ahead],
        scratch_shapes=[
            pltpu.VMEM((width, width), bf16),
            pltpu.VMEM((3, width, count), bf16),
            pltpu.SemaphoreType.DMA((len(ahead),)),
        ],
        compiler_params=params(),
        cost_estimate=pl.CostEstimate(
            flops=12 * count * width * width, bytes_accessed=4 * count * width, transcendentals=0
        ),
        name="grads",
    )(gathered, rates, keys, values, *(in_hbm(array) for array, _ in ahead))


def update_kernel(index, waits, *refs):
    arrived_ref, weights_ref, moment_ref = refs[:3]
    refs = refs[3:]
    rows = weights_ref.shape[0]
    halves = weights_ref.shape[1] // arrived_ref.shape[2]
    gradients = jnp.concatenate(
        [
            jnp.sum(arrived_ref[:, half * rows : (half + 1) * rows, :].astype(f32), axis=0)
            for half in range(halves)
        ],
        axis=1,
    )
    if index == 0:
        squares = jnp.sum(arrived_ref[:, halves * rows :, :].astype(f32), axis=0)
        squares = jnp.concatenate([squares] * halves, axis=1)
        refs[-1][...] = squares
    else:
        squares, refs = refs[0][...], refs[1:]
    square = squares[2 * index : 2 * index + 1, :] + squares[2 * index + 1 : 2 * index + 2, :]
    weights = weights_ref[...]
    moment = momentum_decay * moment_ref[...] + gradients * lax.rsqrt(square)
    stepped = weights - learn_rate * moment
    rescale = jnp.sqrt(
        jnp.sum(weights * weights, axis=1, keepdims=True)
        / (jnp.sum(stepped * stepped, axis=1, keepdims=True) + epsilon)
    )
    weights = stepped * rescale
    rounded = weights.astype(bf16)
    refs = refs[waits:]
    message_ref = refs[0]
    if len(message_ref.shape) == 3:
        message_ref[...] = jnp.broadcast_to(rounded[None], message_ref.shape)
        refs[1][...] = weights
        refs[2][...] = moment
    else:
        message_ref[:rows, :] = rounded
        message_ref[rows:, :] = moment.astype(bf16)


def update(index, arrived, weights, moment, squares, token, leaving):
    rows, width = weights.shape
    given, in_specs = [arrived, weights, moment], [VMEM] * 3
    if index > 0:
        given.append(squares)
        in_specs.append(VMEM)
    waits = token is not None
    if waits:
        given.append(token)
        in_specs.append(VMEM)
    if leaving:
        out_shape = [in_vmem(2 * rows, width, dtype=bf16)]
    else:
        out_shape = [in_vmem(arrived.shape[0], rows, width, dtype=bf16)]
        out_shape += [in_vmem(rows, width)] * 2
    if index == 0:
        out_shape.append(in_vmem(arrived.shape[1] - rows * width // arrived.shape[2], width))
    return pl.pallas_call(
        functools.partial(update_kernel, index, waits),
        in_specs=in_specs,
        out_specs=[VMEM] * len(out_shape),
        out_shape=out_shape,
        compiler_params=params(),
        name="update",
    )(*given)


def enter_kernel(
    first_ref,
    passed_ref,
    fresh_weights_ref,
    fresh_moment_ref,
    wait_ref,
    weights_ref,
    moment_ref,
    message_ref,
):
    rows = weights_ref.shape[0]
    first = first_ref[0] == 0
    passed = passed_ref[...].astype(f32)
    weights = jnp.where(first, fresh_weights_ref[...], passed[:rows])
    weights_ref[...] = weights
    moment_ref[...] = jnp.where(first, fresh_moment_ref[...], passed[rows:])
    message_ref[...] = jnp.broadcast_to(weights.astype(bf16)[None], message_ref.shape)


def enter(first, passed, fresh_weights, fresh_moment, token, parties):
    rows, width = fresh_weights.shape
    return pl.pallas_call(
        enter_kernel,
        in_specs=[SMEM] + [VMEM] * 4,
        out_specs=[VMEM] * 3,
        out_shape=[
            in_vmem(rows, width),
            in_vmem(rows, width),
            in_vmem(parties, rows, width, dtype=bf16),
        ],
        compiler_params=params(),
        name="enter",
    )(first, passed, fresh_weights, fresh_moment, token)


def apply_rows(place, parts, gathered, query_ref, query_rows, out_ref, held_ref, sems):
    length, width = query_rows.shape
    share = width // gathered.shape[0]
    if query_ref is not query_rows:
        (copy,) = started([query_ref], [query_rows], [place], sems)
        copy.wait()
    size = length // parts
    copies = []
    for part in range(parts):
        queries = query_rows[part * size : (part + 1) * size, :]
        pre_gate = dot(queries, matrix(gathered, 0, share), NT)
        pre_up = dot(queries, matrix(gathered, 2, share), NT)
        hidden = (pre_gate * sigmoid(pre_gate) * pre_up).astype(bf16)
        held_ref[part * size : (part + 1) * size, :] = dot(
            hidden, matrix(gathered, 1, share), NT
        ).astype(bf16)
        span = pl.ds(part * size, size)
        copies.append(
            pltpu.make_async_copy(
                held_ref.at[span, :], out_ref.at[*place].at[span, :], sems.at[1 + part]
            )
        )
        copies[-1].start()
    for copy in copies:
        copy.wait()


def apply_kernel(place, staged, waits, extra, when, aliased, hands, parts, gathered_ref, query_ref, *refs):
    wait_ref, refs = (refs[0], refs[1:]) if waits else (None, refs)
    extra_refs, refs = refs[: len(extra)], refs[len(extra) + aliased :]
    out_ref, query_rows, held_ref, sems = refs[0], *refs[-3:]
    if hands:
        refs[1][...] = wait_ref[...] if waits else jnp.zeros_like(refs[1])
    rows_ref = query_ref if staged else query_rows
    if extra == ("instead", "who"):
        gathered_ref = jnp.where(when(extra_refs[1][0]), extra_refs[0][...], gathered_ref[...])
    if extra == ("who",):

        @pl.when(when(extra_refs[0][0]))
        def _():
            apply_rows(place, parts, gathered_ref, query_ref, rows_ref, out_ref, held_ref, sems)

    else:
        apply_rows(place, parts, gathered_ref, query_ref, rows_ref, out_ref, held_ref, sems)


def apply_fast(
    gathered, queries, place, results, shape, token=None, parts=1, instead=None, who=None, when=None, hands=True
):
    count, width = shape[3:]
    staged = len(queries.shape) == 2
    waits = token is not None
    given = [gathered, queries if staged else in_hbm(queries)]
    in_specs = [VMEM, VMEM if staged else HBM]
    extra = ()
    if waits:
        given.append(token)
        in_specs.append(VMEM)
    if instead is not None:
        given.append(instead)
        in_specs.append(VMEM)
        extra += ("instead",)
    if who is not None:
        given.append(who)
        in_specs.append(SMEM)
        extra += ("who",)
    if results is not None:
        given.append(results)
        in_specs.append(HBM)
    out_shape = [jax.ShapeDtypeStruct(shape, bf16)]
    if hands:
        out_shape.append(in_vmem(*token.shape, dtype=token.dtype) if waits else TOKEN)
    results, *handed = pl.pallas_call(
        functools.partial(
            apply_kernel, place, staged, waits, extra, when, int(results is not None), hands, parts
        ),
        in_specs=in_specs,
        out_specs=[HBM] + [VMEM] * hands,
        out_shape=out_shape,
        input_output_aliases={} if results is None else {len(given) - 1: 0},
        scratch_shapes=[
            pltpu.VMEM((count, width), bf16),
            pltpu.VMEM((count, width), bf16),
            pltpu.SemaphoreType.DMA((1 + parts,)),
        ],
        compiler_params=params(),
        cost_estimate=pl.CostEstimate(
            flops=6 * count * width * width, bytes_accessed=4 * count * width, transcendentals=0
        ),
        name="apply",
    )(*given)
    return (results, *handed)


def exchanged(tiles):
    return lax.all_to_all(tiles, TOK, split_axis=0, concat_axis=0, tiled=True)


def passed_on(array):
    length = lax.axis_size("seg")
    return lax.ppermute(array, "seg", [(i, i + 1) for i in range(length - 1)])


def handed_back(array):
    length = lax.axis_size("seg")
    return lax.ppermute(array, "seg", [(i + 1, i) for i in range(length - 1)])


def gathered_by_last(is_last, state, rows, parties):
    width = state.shape[1]
    message = pl.pallas_call(
        copies_kernel,
        in_specs=[VMEM],
        out_specs=VMEM,
        out_shape=in_vmem(parties, rows, width, dtype=bf16),
        compiler_params=params(),
        name="copies",
    )(state)
    return lax.cond(is_last, exchanged, lambda tiles: tiles, message)


def columns_first(state):
    return jnp.swapaxes(state, 1, 2).reshape(-1, state.shape[1])


def rows_first(state, share):
    return jnp.swapaxes(state.reshape(-1, share, state.shape[1]), 1, 2)


def body(
    queries, key_vectors, values, token_rates, fast_weights, momenta, fresh_weights, fresh_momenta
):
    sections, _, blocks, count, _ = queries.shape
    parties = lax.axis_size(TOK)
    share = fast_weights.shape[3]
    place_in_chain = lax.axis_index("seg")
    who = place_in_chain.reshape(1)
    length = lax.axis_size("seg")
    is_last = place_in_chain == length - 1

    def early(segment):
        return (segment % 2 == 1) & (segment != length - 1)

    def late(segment):
        return (segment % 2 == 0) | (segment == length - 1)

    def at_end(segment):
        return segment == length - 1

    weights, moment = columns_first(fast_weights[0]), columns_first(momenta[0])
    fresh_weights, fresh_moment = columns_first(fresh_weights), columns_first(fresh_momenta)
    rows, shape = weights.shape[0], queries.shape
    places = [(section, 0, block) for section in range(sections) for block in range(blocks)]
    message, token = spread(weights, parties)
    *staged, _ = stage(token, who, places[0], (key_vectors, values))
    gathered = exchanged(message)
    results = squares = owed = None
    pending = []
    for index, place in enumerate(places):
        last = index == len(places) - 1
        leaving = not last and place[2] == blocks - 1
        if last:
            ahead = ((queries, place),)
        else:
            ahead = ((key_vectors, places[index + 1]), (values, places[index + 1]))
        message, *staged = grads(
            gathered, token_rates, *staged, (place[0], place[2]), ahead
        )
        arrived = exchanged(message)
        token = None
        if pending and not leaving:
            results, token = apply_fast(*pending.pop(), results, shape)
        message, *state = update(index, arrived, weights, moment, squares, token, leaving)
        if leaving:
            here = pending.pop()
            results, message = apply_fast(*here, results, shape, message, who=who, when=early)
            passed = passed_on(message)
            results, token = apply_fast(*here, results, shape, message, who=who, when=late)
            own = gathered_by_last(is_last, message, rows, parties)
            weights, moment, message = enter(
                who, passed, fresh_weights, fresh_moment, token, parties
            )
            gathered = exchanged(message)
            owed = (handed_back(gathered), queries, place)
        else:
            weights, moment, squares = (*state, squares)[:3]
            gathered = exchanged(message)
            pending.append((gathered, queries, place))
    pending.pop()
    results, token = apply_fast(*owed, results, shape, weights, instead=own, who=who, when=at_end)
    (results,) = apply_fast(
        gathered, staged[0], places[-1], results, shape, token, parts=2, hands=False
    )
    return (results, rows_first(weights, share)[None], rows_first(moment, share)[None])


def solution(mesh):
    finer = Mesh(mesh.devices.reshape(mesh.shape["seg"], 4, 4), ("seg", "tok_0", "tok_1"))
    placed = (
        P(None, "seg", None, TOK, None),
        P(None, "seg", None, TOK, None),
        P(None, "seg", None, TOK, None),
        P(None, "seg", None, TOK),
        P("seg", None, None, TOK),
        P("seg", None, None, TOK),
        P(None, None, TOK),
        P(None, None, TOK),
    )
    return jax.shard_map(
        body,
        mesh=finer,
        in_specs=placed,
        out_specs=(
            P(None, "seg", None, TOK, None),
            P("seg", None, None, TOK),
            P("seg", None, None, TOK),
        ),
        check_vma=False,
    )
```

```python
import functools

import jax
import jax.numpy as jnp
from jax import lax
from jax.experimental import pallas as pl
from jax.experimental.pallas import tpu as pltpu
from jax.sharding import Mesh
from jax.sharding import PartitionSpec as P

TOK = ("tok_0", "tok_1")

momentum_decay = 0.9
learn_rate = 0.05
epsilon = 1e-06

f32, bf16 = jnp.float32, jnp.bfloat16
VMEM_LIMIT = 16 * 1024 * 1024

NN = (((1,), (0,)), ((), ()))
NT = (((1,), (1,)), ((), ()))


def dot(a, b, dims):
    return lax.dot_general(a, b, dims, preferred_element_type=f32)


def sigmoid(a):
    return 0.5 * jnp.tanh(0.5 * a) + 0.5


def matrix(gathered_ref, index, share):
    tiles = gathered_ref[:, index * share : (index + 1) * share, :]
    return tiles.reshape(-1, tiles.shape[-1])


def params(**more):
    return pltpu.CompilerParams(vmem_limit_bytes=VMEM_LIMIT, **more)


def in_vmem(*shape, dtype=f32):
    return pltpu.VMEM(shape, dtype)


VMEM = pl.BlockSpec(memory_space=pltpu.VMEM)
HBM = pl.BlockSpec(memory_space=pltpu.HBM)
SMEM = pl.BlockSpec(memory_space=pltpu.SMEM)


TOKEN = jax.ShapeDtypeStruct((8, 128), f32)


def in_hbm(array):
    return pltpu.with_memory_space_constraint(array, pltpu.HBM)


def started(sources, targets, places, sems):
    copies = [
        pltpu.make_async_copy(source.at[*place], target, sems.at[index])
        for index, (source, target, place) in enumerate(zip(sources, targets, places))
    ]
    for copy in copies:
        copy.start()
    return copies


def rows_in_vmem(array):
    return in_vmem(*array.shape[3:], dtype=array.dtype)


def spread_kernel(weights_ref, message_ref, token_ref, held_ref, sem):
    copy = pltpu.make_async_copy(weights_ref, held_ref, sem)
    copy.start()
    token_ref[...] = jnp.zeros_like(token_ref)
    copy.wait()
    message_ref[...] = jnp.broadcast_to(held_ref[...].astype(bf16)[None], message_ref.shape)


def spread(weights, parties):
    rows, width = weights.shape
    return pl.pallas_call(
        spread_kernel,
        in_specs=[HBM],
        out_specs=[VMEM] * 2,
        out_shape=[in_vmem(parties, rows, width, dtype=bf16), TOKEN],
        scratch_shapes=[pltpu.VMEM((rows, width), f32), pltpu.SemaphoreType.DMA],
        compiler_params=params(),
        name="spread",
    )(in_hbm(weights))


def copies_kernel(state_ref, message_ref):
    rows = message_ref.shape[1]
    message_ref[...] = jnp.broadcast_to(state_ref[:rows, :][None], message_ref.shape)


def stage_kernel(places, *refs):
    count = len(places)
    token_ref, sems = refs[-2:]
    rate_ref = refs[2]
    copies = started(refs[3 : 3 + count], refs[-2 - count : -2], places, sems)
    share, lanes = token_ref.shape
    row = lax.broadcasted_iota(jnp.int32, (share, lanes), 0)
    totals = jnp.zeros((share, lanes), f32)
    blocks = rate_ref.shape[2]
    for index in range(rate_ref.shape[0] * blocks):
        each = index % blocks
        rates = rate_ref[index // blocks, 0, each : each + 1, :]
        square = jnp.sum(rates * rates, axis=1, keepdims=True)
        high = square.astype(bf16).astype(f32)
        totals = jnp.where(row == 2 * index, high, totals)
        totals = jnp.where(row == 2 * index + 1, square - high, totals)
    token_ref[...] = totals.astype(bf16)
    for copy in copies:
        copy.wait()


def stage(token, who, rates, place, arrays, share):
    count = len(arrays)
    return pl.pallas_call(
        functools.partial(stage_kernel, [place] * count),
        in_specs=[VMEM, SMEM, VMEM] + [HBM] * count,
        out_specs=[VMEM] * (count + 1),
        out_shape=[rows_in_vmem(array) for array in arrays]
        + [in_vmem(share, arrays[0].shape[4] // 2, dtype=bf16)],
        scratch_shapes=[pltpu.SemaphoreType.DMA((count,))],
        compiler_params=params(),
        cost_estimate=pl.CostEstimate(
            flops=0, bytes_accessed=count * arrays[0].size, transcendentals=0
        ),
        name="stage",
    )(token, who, rates, *(in_hbm(array) for array in arrays))


def grads_kernel(place, tile, ahead, first, gathered_ref, rate_ref, key_rows, value_rows, *refs):
    later = len(ahead)
    totals_ref, refs = (refs[later], refs[:later] + refs[later + 1 :]) if first else (None, refs)
    message_ref = refs[later]
    left_ref, back_ref, sems = refs[-3:]
    copies = started(refs[:later], refs[later + 1 : 2 * later + 1], ahead, sems)
    parties, rows, lanes = message_ref.shape
    width = gathered_ref.shape[2]
    share = width // parties
    count = key_rows.shape[0]
    section, block = place
    left_ref[...] = matrix(gathered_ref, 1, share).astype(f32).T.astype(bf16)
    gate, up = matrix(gathered_ref, 0, share), matrix(gathered_ref, 2, share)
    for start in range(0, count, tile):
        span = slice(start, start + tile)
        keys, values = key_rows[span, :], value_rows[span, :]
        rate = rate_ref[section, 0, block : block + 1, span]
        pre_gate = dot(gate, keys, NT)
        pre_up = dot(up, keys, NT)
        back = dot(left_ref[...], values, NT) * -rate
        sig = sigmoid(pre_gate)
        active = pre_gate * sig
        slope = sig + active * (1.0 - sig)
        back_ref[0, :, span] = (back * pre_up * slope).astype(bf16)
        back_ref[1, :, span] = (active * pre_up * rate).astype(bf16)
        back_ref[2, :, span] = (back * active).astype(bf16)
    keys, values = key_rows[...], value_rows[...]
    gradients = (
        dot(back_ref[0], keys, NN),
        -dot(back_ref[1], values, NN).T,
        dot(back_ref[2], keys, NN),
    )
    for index, gradient in enumerate(gradients):
        tiles = gradient.astype(bf16).reshape(parties, share, width)
        for half in range(width // lanes):
            start = (3 * half + index) * share
            message_ref[:, start : start + share, :] = tiles[
                :, :, half * lanes : (half + 1) * lanes
            ]
    used = 3 * share * (width // lanes)
    if rows > used:
        message_ref[:, used:, :] = jnp.broadcast_to(
            totals_ref[...][None], (parties, share, lanes)
        )
    for copy in copies:
        copy.wait()


def grads(gathered, rates, keys, values, place, ahead, totals=None):
    parties, _, width = gathered.shape
    share = width // parties
    count = keys.shape[0]
    if totals is not None:
        lanes = width // 2
        rows = 7 * share
    else:
        lanes = width
        rows = 3 * share
    return pl.pallas_call(
        functools.partial(grads_kernel, place, 256, [where for _, where in ahead], totals is not None),
        in_specs=[VMEM] * 4 + [HBM] * len(ahead) + [VMEM] * (totals is not None),
        out_specs=[VMEM] * (1 + len(ahead)),
        out_shape=[in_vmem(parties, rows, lanes, dtype=bf16)]
        + [rows_in_vmem(array) for array, _ in ahead],
        scratch_shapes=[
            pltpu.VMEM((width, width), bf16),
            pltpu.VMEM((3, width, count), bf16),
            pltpu.SemaphoreType.DMA((len(ahead),)),
        ],
        compiler_params=params(),
        cost_estimate=pl.CostEstimate(
            flops=12 * count * width * width, bytes_accessed=4 * count * width, transcendentals=0
        ),
        name="grads",
    )(gathered, rates, keys, values, *(in_hbm(array) for array, _ in ahead), *(() if totals is None else (totals,)))


def update_kernel(index, waits, *refs):
    arrived_ref, weights_ref, moment_ref = refs[:3]
    refs = refs[3:]
    rows = weights_ref.shape[0]
    halves = weights_ref.shape[1] // arrived_ref.shape[2]
    gradients = jnp.concatenate(
        [
            jnp.sum(arrived_ref[:, half * rows : (half + 1) * rows, :].astype(f32), axis=0)
            for half in range(halves)
        ],
        axis=1,
    )
    if index == 0:
        squares = jnp.sum(arrived_ref[:, halves * rows :, :].astype(f32), axis=0)
        squares = jnp.concatenate([squares] * halves, axis=1)
        refs[-1][...] = squares
    else:
        squares, refs = refs[0][...], refs[1:]
    square = squares[2 * index : 2 * index + 1, :] + squares[2 * index + 1 : 2 * index + 2, :]
    weights = weights_ref[...]
    moment = momentum_decay * moment_ref[...] + gradients * lax.rsqrt(square)
    stepped = weights - learn_rate * moment
    rescale = jnp.sqrt(
        jnp.sum(weights * weights, axis=1, keepdims=True)
        / (jnp.sum(stepped * stepped, axis=1, keepdims=True) + epsilon)
    )
    weights = stepped * rescale
    rounded = weights.astype(bf16)
    refs = refs[waits:]
    message_ref = refs[0]
    if len(message_ref.shape) == 3:
        message_ref[...] = jnp.broadcast_to(rounded[None], message_ref.shape)
        refs[1][...] = weights
        refs[2][...] = moment
    else:
        message_ref[:rows, :] = rounded
        message_ref[rows:, :] = moment.astype(bf16)


def update(index, arrived, weights, moment, squares, token, leaving):
    rows, width = weights.shape
    given, in_specs = [arrived, weights, moment], [VMEM] * 3
    if index > 0:
        given.append(squares)
        in_specs.append(VMEM)
    waits = token is not None
    if waits:
        given.append(token)
        in_specs.append(VMEM)
    if leaving:
        out_shape = [in_vmem(2 * rows, width, dtype=bf16)]
    else:
        out_shape = [in_vmem(arrived.shape[0], rows, width, dtype=bf16)]
        out_shape += [in_vmem(rows, width)] * 2
    if index == 0:
        out_shape.append(in_vmem(arrived.shape[1] - rows * width // arrived.shape[2], width))
    return pl.pallas_call(
        functools.partial(update_kernel, index, waits),
        in_specs=in_specs,
        out_specs=[VMEM] * len(out_shape),
        out_shape=out_shape,
        compiler_params=params(),
        name="update",
    )(*given)


def enter_kernel(
    first_ref,
    passed_ref,
    fresh_weights_ref,
    fresh_moment_ref,
    wait_ref,
    weights_ref,
    moment_ref,
    message_ref,
):
    rows = weights_ref.shape[0]
    first = first_ref[0] == 0
    passed = passed_ref[...].astype(f32)
    weights = jnp.where(first, fresh_weights_ref[...], passed[:rows])
    weights_ref[...] = weights
    moment_ref[...] = jnp.where(first, fresh_moment_ref[...], passed[rows:])
    message_ref[...] = jnp.broadcast_to(weights.astype(bf16)[None], message_ref.shape)


def enter(first, passed, fresh_weights, fresh_moment, token, parties):
    rows, width = fresh_weights.shape
    return pl.pallas_call(
        enter_kernel,
        in_specs=[SMEM] + [VMEM] * 4,
        out_specs=[VMEM] * 3,
        out_shape=[
            in_vmem(rows, width),
            in_vmem(rows, width),
            in_vmem(parties, rows, width, dtype=bf16),
        ],
        compiler_params=params(),
        name="enter",
    )(first, passed, fresh_weights, fresh_moment, token)


def apply_rows(place, parts, gathered, query_ref, query_rows, out_ref, held_ref, sems):
    length, width = query_rows.shape
    share = width // gathered.shape[0]
    if query_ref is not query_rows:
        (copy,) = started([query_ref], [query_rows], [place], sems)
        copy.wait()
    size = length // parts
    copies = []
    for part in range(parts):
        queries = query_rows[part * size : (part + 1) * size, :]
        pre_gate = dot(queries, matrix(gathered, 0, share), NT)
        pre_up = dot(queries, matrix(gathered, 2, share), NT)
        hidden = (pre_gate * sigmoid(pre_gate) * pre_up).astype(bf16)
        held_ref[part * size : (part + 1) * size, :] = dot(
            hidden, matrix(gathered, 1, share), NT
        ).astype(bf16)
        span = pl.ds(part * size, size)
        copies.append(
            pltpu.make_async_copy(
                held_ref.at[span, :], out_ref.at[*place].at[span, :], sems.at[1 + part]
            )
        )
        copies[-1].start()
    for copy in copies:
        copy.wait()


def apply_kernel(place, staged, waits, extra, when, aliased, hands, parts, gathered_ref, query_ref, *refs):
    wait_ref, refs = (refs[0], refs[1:]) if waits else (None, refs)
    extra_refs, refs = refs[: len(extra)], refs[len(extra) + aliased :]
    out_ref, query_rows, held_ref, sems = refs[0], *refs[-3:]
    if hands:
        refs[1][...] = wait_ref[...] if waits else jnp.zeros_like(refs[1])
    rows_ref = query_ref if staged else query_rows
    if extra == ("instead", "who"):
        gathered_ref = jnp.where(when(extra_refs[1][0]), extra_refs[0][...], gathered_ref[...])
    if extra == ("who",):

        @pl.when(when(extra_refs[0][0]))
        def _():
            apply_rows(place, parts, gathered_ref, query_ref, rows_ref, out_ref, held_ref, sems)

    else:
        apply_rows(place, parts, gathered_ref, query_ref, rows_ref, out_ref, held_ref, sems)


def apply_fast(
    gathered, queries, place, results, shape, token=None, parts=1, instead=None, who=None, when=None, hands=True
):
    count, width = shape[3:]
    staged = len(queries.shape) == 2
    waits = token is not None
    given = [gathered, queries if staged else in_hbm(queries)]
    in_specs = [VMEM, VMEM if staged else HBM]
    extra = ()
    if waits:
        given.append(token)
        in_specs.append(VMEM)
    if instead is not None:
        given.append(instead)
        in_specs.append(VMEM)
        extra += ("instead",)
    if who is not None:
        given.append(who)
        in_specs.append(SMEM)
        extra += ("who",)
    if results is not None:
        given.append(results)
        in_specs.append(HBM)
    out_shape = [jax.ShapeDtypeStruct(shape, bf16)]
    if hands:
        out_shape.append(in_vmem(*token.shape, dtype=token.dtype) if waits else TOKEN)
    results, *handed = pl.pallas_call(
        functools.partial(
            apply_kernel, place, staged, waits, extra, when, int(results is not None), hands, parts
        ),
        in_specs=in_specs,
        out_specs=[HBM] + [VMEM] * hands,
        out_shape=out_shape,
        input_output_aliases={} if results is None else {len(given) - 1: 0},
        scratch_shapes=[
            pltpu.VMEM((count, width), bf16),
            pltpu.VMEM((count, width), bf16),
            pltpu.SemaphoreType.DMA((1 + parts,)),
        ],
        compiler_params=params(),
        cost_estimate=pl.CostEstimate(
            flops=6 * count * width * width, bytes_accessed=4 * count * width, transcendentals=0
        ),
        name="apply",
    )(*given)
    return (results, *handed)


def exchanged(tiles):
    return lax.all_to_all(tiles, TOK, split_axis=0, concat_axis=0, tiled=True)


def passed_on(array):
    length = lax.axis_size("seg")
    return lax.ppermute(array, "seg", [(i, i + 1) for i in range(length - 1)])


def handed_back(array):
    length = lax.axis_size("seg")
    return lax.ppermute(array, "seg", [(i + 1, i) for i in range(length - 1)])


def gathered_by_last(is_last, state, rows, parties):
    width = state.shape[1]
    message = pl.pallas_call(
        copies_kernel,
        in_specs=[VMEM],
        out_specs=VMEM,
        out_shape=in_vmem(parties, rows, width, dtype=bf16),
        compiler_params=params(),
        name="copies",
    )(state)
    return lax.cond(is_last, exchanged, lambda tiles: tiles, message)


def columns_first(state):
    return jnp.swapaxes(state, 1, 2).reshape(-1, state.shape[1])


def rows_first(state, share):
    return jnp.swapaxes(state.reshape(-1, share, state.shape[1]), 1, 2)


def body(
    queries, key_vectors, values, token_rates, fast_weights, momenta, fresh_weights, fresh_momenta
):
    sections, _, blocks, count, _ = queries.shape
    parties = lax.axis_size(TOK)
    share = fast_weights.shape[3]
    place_in_chain = lax.axis_index("seg")
    who = place_in_chain.reshape(1)
    length = lax.axis_size("seg")
    is_last = place_in_chain == length - 1

    def early(segment):
        return (segment % 2 == 1) & (segment != length - 1)

    def late(segment):
        return (segment % 2 == 0) | (segment == length - 1)

    def at_end(segment):
        return segment == length - 1

    weights, moment = columns_first(fast_weights[0]), columns_first(momenta[0])
    fresh_weights, fresh_moment = columns_first(fresh_weights), columns_first(fresh_momenta)
    rows, shape = weights.shape[0], queries.shape
    places = [(section, 0, block) for section in range(sections) for block in range(blocks)]
    message, token = spread(weights, parties)
    *staged, totals = stage(token, who, token_rates, places[0], (key_vectors, values), share)
    gathered = exchanged(message)
    results = squares = owed = None
    pending = []
    for index, place in enumerate(places):
        last = index == len(places) - 1
        leaving = not last and place[2] == blocks - 1
        if last:
            ahead = ((queries, place),)
        else:
            ahead = ((key_vectors, places[index + 1]), (values, places[index + 1]))
        message, *staged = grads(
            gathered,
            token_rates,
            *staged,
            (place[0], place[2]),
            ahead,
            totals if index == 0 else None,
        )
        arrived = exchanged(message)
        token = None
        if pending and not leaving:
            results, token = apply_fast(*pending.pop(), results, shape)
        message, *state = update(index, arrived, weights, moment, squares, token, leaving)
        if leaving:
            here = pending.pop()
            results, message = apply_fast(*here, results, shape, message, who=who, when=early)
            passed = passed_on(message)
            results, token = apply_fast(*here, results, shape, message, who=who, when=late)
            own = gathered_by_last(is_last, message, rows, parties)
            weights, moment, message = enter(
                who, passed, fresh_weights, fresh_moment, token, parties
            )
            gathered = exchanged(message)
            owed = (handed_back(gathered), queries, place)
        else:
            weights, moment, squares = (*state, squares)[:3]
            gathered = exchanged(message)
            pending.append((gathered, queries, place))
    pending.pop()
    results, token = apply_fast(*owed, results, shape, weights, instead=own, who=who, when=at_end)
    (results,) = apply_fast(
        gathered, staged[0], places[-1], results, shape, token, parts=2, hands=False
    )
    return (results, rows_first(weights, share)[None], rows_first(moment, share)[None])


def solution(mesh):
    finer = Mesh(mesh.devices.reshape(mesh.shape["seg"], 4, 4), ("seg", "tok_0", "tok_1"))
    placed = (
        P(None, "seg", None, TOK, None),
        P(None, "seg", None, TOK, None),
        P(None, "seg", None, TOK, None),
        P(None, "seg", None, TOK),
        P("seg", None, None, TOK),
        P("seg", None, None, TOK),
        P(None, None, TOK),
        P(None, None, TOK),
    )
    return jax.shard_map(
        body,
        mesh=finer,
        in_specs=placed,
        out_specs=(
            P(None, "seg", None, TOK, None),
            P("seg", None, None, TOK),
            P("seg", None, None, TOK),
        ),
        check_vma=False,
    )
```

```python
import functools

import jax
import jax.numpy as jnp
from jax import lax
from jax.experimental import pallas as pl
from jax.experimental.pallas import tpu as pltpu
from jax.sharding import Mesh
from jax.sharding import PartitionSpec as P

TOK = ("tok_0", "tok_1")

momentum_decay = 0.9
learn_rate = 0.05
epsilon = 1e-06

f32, bf16 = jnp.float32, jnp.bfloat16
VMEM_LIMIT = 16 * 1024 * 1024

NN = (((1,), (0,)), ((), ()))
NT = (((1,), (1,)), ((), ()))


def dot(a, b, dims):
    return lax.dot_general(a, b, dims, preferred_element_type=f32)


def sigmoid(a):
    return 0.5 * jnp.tanh(0.5 * a) + 0.5


def matrix(gathered_ref, index, share):
    tiles = gathered_ref[:, index * share : (index + 1) * share, :]
    return tiles.reshape(-1, tiles.shape[-1])


def params(**more):
    return pltpu.CompilerParams(vmem_limit_bytes=VMEM_LIMIT, **more)


def in_vmem(*shape, dtype=f32):
    return pltpu.VMEM(shape, dtype)


VMEM = pl.BlockSpec(memory_space=pltpu.VMEM)
HBM = pl.BlockSpec(memory_space=pltpu.HBM)
SMEM = pl.BlockSpec(memory_space=pltpu.SMEM)


TOKEN = jax.ShapeDtypeStruct((8, 128), f32)


def in_hbm(array):
    return pltpu.with_memory_space_constraint(array, pltpu.HBM)


def started(sources, targets, places, sems):
    copies = [
        pltpu.make_async_copy(source.at[*place], target, sems.at[index])
        for index, (source, target, place) in enumerate(zip(sources, targets, places))
    ]
    for copy in copies:
        copy.start()
    return copies


def rows_in_vmem(array):
    return in_vmem(*array.shape[3:], dtype=array.dtype)


def spread_kernel(weights_ref, message_ref, token_ref, held_ref, sem):
    copy = pltpu.make_async_copy(weights_ref, held_ref, sem)
    copy.start()
    token_ref[...] = jnp.zeros_like(token_ref)
    copy.wait()
    message_ref[...] = jnp.broadcast_to(held_ref[...].astype(bf16)[None], message_ref.shape)


def spread(weights, parties):
    rows, width = weights.shape
    return pl.pallas_call(
        spread_kernel,
        in_specs=[HBM],
        out_specs=[VMEM] * 2,
        out_shape=[in_vmem(parties, rows, width, dtype=bf16), TOKEN],
        scratch_shapes=[pltpu.VMEM((rows, width), f32), pltpu.SemaphoreType.DMA],
        compiler_params=params(),
        name="spread",
    )(in_hbm(weights))


def copies_kernel(state_ref, message_ref):
    rows = message_ref.shape[1]
    message_ref[...] = jnp.broadcast_to(state_ref[:rows, :][None], message_ref.shape)


def stage_kernel(places, *refs):
    count = len(places)
    token_ref, sems = refs[-2:]
    rate_ref = refs[2]
    copies = started(refs[3 : 3 + count], refs[-2 - count : -2], places, sems)
    share, lanes = token_ref.shape
    row = lax.broadcasted_iota(jnp.int32, (share, lanes), 0)
    totals = jnp.zeros((share, lanes), f32)
    blocks = rate_ref.shape[2]
    for index in range(rate_ref.shape[0] * blocks):
        each = index % blocks
        rates = rate_ref[index // blocks, 0, each : each + 1, :]
        square = jnp.sum(rates * rates, axis=1, keepdims=True)
        high = square.astype(bf16).astype(f32)
        totals = jnp.where(row == 2 * index, high, totals)
        totals = jnp.where(row == 2 * index + 1, square - high, totals)
    token_ref[...] = totals.astype(bf16)
    for copy in copies:
        copy.wait()


def stage(token, who, rates, place, arrays, share):
    count = len(arrays)
    return pl.pallas_call(
        functools.partial(stage_kernel, [place] * count),
        in_specs=[VMEM, SMEM, VMEM] + [HBM] * count,
        out_specs=[VMEM] * (count + 1),
        out_shape=[rows_in_vmem(array) for array in arrays]
        + [in_vmem(share, arrays[0].shape[4] // 2, dtype=bf16)],
        scratch_shapes=[pltpu.SemaphoreType.DMA((count,))],
        compiler_params=params(),
        cost_estimate=pl.CostEstimate(
            flops=0, bytes_accessed=count * arrays[0].size, transcendentals=0
        ),
        name="stage",
    )(token, who, rates, *(in_hbm(array) for array in arrays))


def grads_kernel(place, tile, ahead, first, gathered_ref, rate_ref, key_rows, value_rows, *refs):
    later = len(ahead)
    totals_ref, refs = (refs[later], refs[:later] + refs[later + 1 :]) if first else (None, refs)
    message_ref = refs[later]
    left_ref, back_ref, sems = refs[-3:]
    copies = started(refs[:later], refs[later + 1 : 2 * later + 1], ahead, sems)
    parties, rows, lanes = message_ref.shape
    width = gathered_ref.shape[2]
    share = width // parties
    count = key_rows.shape[0]
    section, block = place
    left_ref[...] = matrix(gathered_ref, 1, share).astype(f32).T.astype(bf16)
    gate, up = matrix(gathered_ref, 0, share), matrix(gathered_ref, 2, share)
    for start in range(0, count, tile):
        span = slice(start, start + tile)
        keys, values = key_rows[span, :], value_rows[span, :]
        rate = rate_ref[section, 0, block : block + 1, span]
        pre_gate = dot(gate, keys, NT)
        pre_up = dot(up, keys, NT)
        back = dot(left_ref[...], values, NT) * -rate
        sig = sigmoid(pre_gate)
        active = pre_gate * sig
        slope = sig + active * (1.0 - sig)
        back_ref[0, :, span] = (back * pre_up * slope).astype(bf16)
        back_ref[1, :, span] = (active * pre_up * rate).astype(bf16)
        back_ref[2, :, span] = (back * active).astype(bf16)
    keys, values = key_rows[...], value_rows[...]
    gradients = (
        dot(back_ref[0], keys, NN),
        -dot(back_ref[1], values, NN).T,
        dot(back_ref[2], keys, NN),
    )
    for index, gradient in enumerate(gradients):
        tiles = gradient.astype(bf16).reshape(parties, share, width)
        for half in range(width // lanes):
            start = (3 * half + index) * share
            message_ref[:, start : start + share, :] = tiles[
                :, :, half * lanes : (half + 1) * lanes
            ]
    used = 3 * share * (width // lanes)
    if rows > used:
        message_ref[:, used:, :] = jnp.broadcast_to(
            totals_ref[...][None], (parties, share, lanes)
        )
    for copy in copies:
        copy.wait()


def grads(gathered, rates, keys, values, place, ahead, totals=None):
    parties, _, width = gathered.shape
    share = width // parties
    count = keys.shape[0]
    if totals is not None:
        lanes = width // 2
        rows = 7 * share
    else:
        lanes = width
        rows = 3 * share
    return pl.pallas_call(
        functools.partial(grads_kernel, place, 256, [where for _, where in ahead], totals is not None),
        in_specs=[VMEM] * 4 + [HBM] * len(ahead) + [VMEM] * (totals is not None),
        out_specs=[VMEM] * (1 + len(ahead)),
        out_shape=[in_vmem(parties, rows, lanes, dtype=bf16)]
        + [rows_in_vmem(array) for array, _ in ahead],
        scratch_shapes=[
            pltpu.VMEM((width, width), bf16),
            pltpu.VMEM((3, width, count), bf16),
            pltpu.SemaphoreType.DMA((len(ahead),)),
        ],
        compiler_params=params(),
        cost_estimate=pl.CostEstimate(
            flops=12 * count * width * width, bytes_accessed=4 * count * width, transcendentals=0
        ),
        name="grads",
    )(gathered, rates, keys, values, *(in_hbm(array) for array, _ in ahead), *(() if totals is None else (totals,)))


def update_kernel(index, waits, *refs):
    arrived_ref, weights_ref, moment_ref = refs[:3]
    refs = refs[3:]
    rows = weights_ref.shape[0]
    halves = weights_ref.shape[1] // arrived_ref.shape[2]
    gradients = jnp.concatenate(
        [
            jnp.sum(arrived_ref[:, half * rows : (half + 1) * rows, :].astype(f32), axis=0)
            for half in range(halves)
        ],
        axis=1,
    )
    if index == 0:
        squares = jnp.sum(arrived_ref[:, halves * rows :, :].astype(f32), axis=0)
        squares = jnp.concatenate([squares] * halves, axis=1)
        refs[-1][...] = squares
    else:
        squares, refs = refs[0][...], refs[1:]
    square = squares[2 * index : 2 * index + 1, :] + squares[2 * index + 1 : 2 * index + 2, :]
    weights = weights_ref[...]
    moment = momentum_decay * moment_ref[...] + gradients * lax.rsqrt(square)
    stepped = weights - learn_rate * moment
    rescale = jnp.sqrt(
        jnp.sum(weights * weights, axis=1, keepdims=True)
        / (jnp.sum(stepped * stepped, axis=1, keepdims=True) + epsilon)
    )
    weights = stepped * rescale
    rounded = weights.astype(bf16)
    refs = refs[waits:]
    message_ref = refs[0]
    if len(message_ref.shape) == 3:
        message_ref[...] = jnp.broadcast_to(rounded[None], message_ref.shape)
        refs[1][...] = weights
        refs[2][...] = moment
    else:
        message_ref[:rows, :] = rounded
        message_ref[rows:, :] = moment.astype(bf16)


def update(index, arrived, weights, moment, squares, token, leaving):
    rows, width = weights.shape
    given, in_specs = [arrived, weights, moment], [VMEM] * 3
    if index > 0:
        given.append(squares)
        in_specs.append(VMEM)
    waits = token is not None
    if waits:
        given.append(token)
        in_specs.append(VMEM)
    if leaving:
        out_shape = [in_vmem(2 * rows, width, dtype=bf16)]
    else:
        out_shape = [in_vmem(arrived.shape[0], rows, width, dtype=bf16)]
        out_shape += [in_vmem(rows, width)] * 2
    if index == 0:
        out_shape.append(in_vmem(arrived.shape[1] - rows * width // arrived.shape[2], width))
    return pl.pallas_call(
        functools.partial(update_kernel, index, waits),
        in_specs=in_specs,
        out_specs=[VMEM] * len(out_shape),
        out_shape=out_shape,
        compiler_params=params(),
        name="update",
    )(*given)


def enter_kernel(
    first_ref,
    passed_ref,
    fresh_weights_ref,
    fresh_moment_ref,
    wait_ref,
    weights_ref,
    moment_ref,
    message_ref,
):
    rows = weights_ref.shape[0]
    first = first_ref[0] == 0
    passed = passed_ref[...].astype(f32)
    weights = jnp.where(first, fresh_weights_ref[...], passed[:rows])
    weights_ref[...] = weights
    moment_ref[...] = jnp.where(first, fresh_moment_ref[...], passed[rows:])
    message_ref[...] = jnp.broadcast_to(weights.astype(bf16)[None], message_ref.shape)


def enter(first, passed, fresh_weights, fresh_moment, token, parties):
    rows, width = fresh_weights.shape
    return pl.pallas_call(
        enter_kernel,
        in_specs=[SMEM] + [VMEM] * 4,
        out_specs=[VMEM] * 3,
        out_shape=[
            in_vmem(rows, width),
            in_vmem(rows, width),
            in_vmem(parties, rows, width, dtype=bf16),
        ],
        compiler_params=params(),
        name="enter",
    )(first, passed, fresh_weights, fresh_moment, token)


def apply_rows(place, parts, gathered, query_ref, query_rows, out_ref, held_ref, sems):
    length, width = query_rows.shape
    share = width // gathered.shape[0]
    if query_ref is not query_rows:
        (copy,) = started([query_ref], [query_rows], [place], sems)
        copy.wait()
    size = length // parts
    copies = []
    for part in range(parts):
        queries = query_rows[part * size : (part + 1) * size, :]
        pre_gate = dot(queries, matrix(gathered, 0, share), NT)
        pre_up = dot(queries, matrix(gathered, 2, share), NT)
        hidden = (pre_gate * sigmoid(pre_gate) * pre_up).astype(bf16)
        held_ref[part * size : (part + 1) * size, :] = dot(
            hidden, matrix(gathered, 1, share), NT
        ).astype(bf16)
        span = pl.ds(part * size, size)
        copies.append(
            pltpu.make_async_copy(
                held_ref.at[span, :], out_ref.at[*place].at[span, :], sems.at[1 + part]
            )
        )
        copies[-1].start()
    for copy in copies:
        copy.wait()


def apply_kernel(place, staged, waits, extra, when, aliased, hands, parts, gathered_ref, query_ref, *refs):
    wait_ref, refs = (refs[0], refs[1:]) if waits else (None, refs)
    extra_refs, refs = refs[: len(extra)], refs[len(extra) + aliased :]
    out_ref, query_rows, held_ref, sems = refs[0], *refs[-3:]
    if hands:
        refs[1][...] = wait_ref[...] if waits else jnp.zeros_like(refs[1])
    rows_ref = query_ref if staged else query_rows
    if extra == ("instead", "who"):
        gathered_ref = jnp.where(when(extra_refs[1][0]), extra_refs[0][...], gathered_ref[...])
    if extra == ("who",):

        @pl.when(when(extra_refs[0][0]))
        def _():
            apply_rows(place, parts, gathered_ref, query_ref, rows_ref, out_ref, held_ref, sems)

    else:
        apply_rows(place, parts, gathered_ref, query_ref, rows_ref, out_ref, held_ref, sems)


def apply_fast(
    gathered, queries, place, results, shape, token=None, parts=1, instead=None, who=None, when=None, hands=True
):
    count, width = shape[3:]
    staged = len(queries.shape) == 2
    waits = token is not None
    given = [gathered, queries if staged else in_hbm(queries)]
    in_specs = [VMEM, VMEM if staged else HBM]
    extra = ()
    if waits:
        given.append(token)
        in_specs.append(VMEM)
    if instead is not None:
        given.append(instead)
        in_specs.append(VMEM)
        extra += ("instead",)
    if who is not None:
        given.append(who)
        in_specs.append(SMEM)
        extra += ("who",)
    if results is not None:
        given.append(results)
        in_specs.append(HBM)
    out_shape = [jax.ShapeDtypeStruct(shape, bf16)]
    if hands:
        out_shape.append(in_vmem(*token.shape, dtype=token.dtype) if waits else TOKEN)
    results, *handed = pl.pallas_call(
        functools.partial(
            apply_kernel, place, staged, waits, extra, when, int(results is not None), hands, parts
        ),
        in_specs=in_specs,
        out_specs=[HBM] + [VMEM] * hands,
        out_shape=out_shape,
        input_output_aliases={} if results is None else {len(given) - 1: 0},
        scratch_shapes=[
            pltpu.VMEM((count, width), bf16),
            pltpu.VMEM((count, width), bf16),
            pltpu.SemaphoreType.DMA((1 + parts,)),
        ],
        compiler_params=params(),
        cost_estimate=pl.CostEstimate(
            flops=6 * count * width * width, bytes_accessed=4 * count * width, transcendentals=0
        ),
        name="apply",
    )(*given)
    return (results, *handed)


def exchanged(tiles):
    return lax.all_to_all(tiles, TOK, split_axis=0, concat_axis=0, tiled=True)


def passed_on(array):
    length = lax.axis_size("seg")
    return lax.ppermute(array, "seg", [(i, i + 1) for i in range(length - 1)])


def handed_back(array):
    length = lax.axis_size("seg")
    return lax.ppermute(array, "seg", [(i + 1, i) for i in range(length - 1)])


def gathered_by_last(is_last, state, rows, parties):
    width = state.shape[1]
    message = pl.pallas_call(
        copies_kernel,
        in_specs=[VMEM],
        out_specs=VMEM,
        out_shape=in_vmem(parties, rows, width, dtype=bf16),
        compiler_params=params(),
        name="copies",
    )(state)
    return lax.cond(is_last, exchanged, lambda tiles: tiles, message)


def columns_first(state):
    return jnp.swapaxes(state, 1, 2).reshape(-1, state.shape[1])


def rows_first(state, share):
    return jnp.swapaxes(state.reshape(-1, share, state.shape[1]), 1, 2)


def body(
    queries, key_vectors, values, token_rates, fast_weights, momenta, fresh_weights, fresh_momenta
):
    sections, _, blocks, count, _ = queries.shape
    parties = lax.axis_size(TOK)
    share = fast_weights.shape[3]
    place_in_chain = lax.axis_index("seg")
    who = place_in_chain.reshape(1)
    length = lax.axis_size("seg")
    is_last = place_in_chain == length - 1

    def early(segment):
        return (segment % 2 == 1) & (segment != length - 1)

    def late(segment):
        return (segment % 2 == 0) | (segment == length - 1)

    def at_end(segment):
        return segment == length - 1

    weights, moment = columns_first(fast_weights[0]), columns_first(momenta[0])
    fresh_weights, fresh_moment = columns_first(fresh_weights), columns_first(fresh_momenta)
    rows, shape = weights.shape[0], queries.shape
    places = [(section, 0, block) for section in range(sections) for block in range(blocks)]
    message, token = spread(weights, parties)
    *staged, totals = stage(token, who, token_rates, places[0], (key_vectors, values), share)
    gathered = exchanged(message)
    results = squares = owed = None
    pending = []
    for index, place in enumerate(places):
        last = index == len(places) - 1
        leaving = not last and place[2] == blocks - 1
        if last:
            ahead = ((queries, place),)
        else:
            ahead = ((key_vectors, places[index + 1]), (values, places[index + 1]))
        message, *staged = grads(
            gathered,
            token_rates,
            *staged,
            (place[0], place[2]),
            ahead,
            totals if index == 0 else None,
        )
        arrived = exchanged(message)
        token = None
        if pending and not leaving:
            results, token = apply_fast(*pending.pop(), results, shape, owed[0])
            owed = (handed_back(token), *owed[1:])
        message, *state = update(index, arrived, weights, moment, squares, token, leaving)
        if leaving:
            here = pending.pop()
            results, message = apply_fast(*here, results, shape, message, who=who, when=early)
            passed = passed_on(message)
            results, token = apply_fast(*here, results, shape, message, who=who, when=late)
            own = gathered_by_last(is_last, message, rows, parties)
            weights, moment, message = enter(
                who, passed, fresh_weights, fresh_moment, token, parties
            )
            gathered = exchanged(message)
            owed = (gathered, queries, place)
        else:
            weights, moment, squares = (*state, squares)[:3]
            gathered = exchanged(message)
            pending.append((gathered, queries, place))
    pending.pop()
    results, token = apply_fast(*owed, results, shape, weights, instead=own, who=who, when=at_end)
    (results,) = apply_fast(
        gathered, staged[0], places[-1], results, shape, token, parts=2, hands=False
    )
    return (results, rows_first(weights, share)[None], rows_first(moment, share)[None])


def solution(mesh):
    finer = Mesh(mesh.devices.reshape(mesh.shape["seg"], 4, 4), ("seg", "tok_0", "tok_1"))
    placed = (
        P(None, "seg", None, TOK, None),
        P(None, "seg", None, TOK, None),
        P(None, "seg", None, TOK, None),
        P(None, "seg", None, TOK),
        P("seg", None, None, TOK),
        P("seg", None, None, TOK),
        P(None, None, TOK),
        P(None, None, TOK),
    )
    return jax.shard_map(
        body,
        mesh=finer,
        in_specs=placed,
        out_specs=(
            P(None, "seg", None, TOK, None),
            P("seg", None, None, TOK),
            P("seg", None, None, TOK),
        ),
        check_vma=False,
    )
```

```python
import functools

import jax
import jax.numpy as jnp
from jax import lax
from jax.experimental import pallas as pl
from jax.experimental.pallas import tpu as pltpu
from jax.sharding import Mesh
from jax.sharding import PartitionSpec as P

TOK = ("tok_0", "tok_1")

momentum_decay = 0.9
learn_rate = 0.05
epsilon = 1e-06

f32, bf16 = jnp.float32, jnp.bfloat16
VMEM_LIMIT = 16 * 1024 * 1024

NN = (((1,), (0,)), ((), ()))
NT = (((1,), (1,)), ((), ()))


def dot(a, b, dims):
    return lax.dot_general(a, b, dims, preferred_element_type=f32)


def sigmoid(a):
    return 0.5 * jnp.tanh(0.5 * a) + 0.5


def matrix(gathered_ref, index, share):
    tiles = gathered_ref[:, index * share : (index + 1) * share, :]
    return tiles.reshape(-1, tiles.shape[-1])


def params(**more):
    return pltpu.CompilerParams(vmem_limit_bytes=VMEM_LIMIT, **more)


def in_vmem(*shape, dtype=f32):
    return pltpu.VMEM(shape, dtype)


VMEM = pl.BlockSpec(memory_space=pltpu.VMEM)
HBM = pl.BlockSpec(memory_space=pltpu.HBM)
SMEM = pl.BlockSpec(memory_space=pltpu.SMEM)


TOKEN = jax.ShapeDtypeStruct((8, 128), f32)


def in_hbm(array):
    return pltpu.with_memory_space_constraint(array, pltpu.HBM)


def started(sources, targets, places, sems):
    copies = [
        pltpu.make_async_copy(source.at[*place], target, sems.at[index])
        for index, (source, target, place) in enumerate(zip(sources, targets, places))
    ]
    for copy in copies:
        copy.start()
    return copies


def rows_in_vmem(array):
    return in_vmem(*array.shape[3:], dtype=array.dtype)


def spread_kernel(weights_ref, message_ref, token_ref, held_ref, sem):
    copy = pltpu.make_async_copy(weights_ref, held_ref, sem)
    copy.start()
    token_ref[...] = jnp.zeros_like(token_ref)
    copy.wait()
    message_ref[...] = jnp.broadcast_to(held_ref[...].astype(bf16)[None], message_ref.shape)


def spread(weights, parties):
    rows, width = weights.shape
    return pl.pallas_call(
        spread_kernel,
        in_specs=[HBM],
        out_specs=[VMEM] * 2,
        out_shape=[in_vmem(parties, rows, width, dtype=bf16), TOKEN],
        scratch_shapes=[pltpu.VMEM((rows, width), f32), pltpu.SemaphoreType.DMA],
        compiler_params=params(),
        name="spread",
    )(in_hbm(weights))


def copies_kernel(state_ref, message_ref):
    rows = message_ref.shape[1]
    message_ref[...] = jnp.broadcast_to(state_ref[:rows, :][None], message_ref.shape)


def stage_kernel(places, *refs):
    count = len(places)
    token_ref, sems = refs[-2:]
    rate_ref = refs[2]
    copies = started(refs[3 : 3 + count], refs[-2 - count : -2], places, sems)
    share, lanes = token_ref.shape
    row = lax.broadcasted_iota(jnp.int32, (share, lanes), 0)
    totals = jnp.zeros((share, lanes), f32)
    blocks = rate_ref.shape[2]
    for index in range(rate_ref.shape[0] * blocks):
        each = index % blocks
        rates = rate_ref[index // blocks, 0, each : each + 1, :]
        square = jnp.sum(rates * rates, axis=1, keepdims=True)
        high = square.astype(bf16).astype(f32)
        totals = jnp.where(row == 2 * index, high, totals)
        totals = jnp.where(row == 2 * index + 1, square - high, totals)
    token_ref[...] = totals.astype(bf16)
    for copy in copies:
        copy.wait()


def stage(token, who, rates, place, arrays, share):
    count = len(arrays)
    return pl.pallas_call(
        functools.partial(stage_kernel, [place] * count),
        in_specs=[VMEM, SMEM, VMEM] + [HBM] * count,
        out_specs=[VMEM] * (count + 1),
        out_shape=[rows_in_vmem(array) for array in arrays]
        + [in_vmem(share, arrays[0].shape[4] // 2, dtype=bf16)],
        scratch_shapes=[pltpu.SemaphoreType.DMA((count,))],
        compiler_params=params(),
        cost_estimate=pl.CostEstimate(
            flops=0, bytes_accessed=count * arrays[0].size, transcendentals=0
        ),
        name="stage",
    )(token, who, rates, *(in_hbm(array) for array in arrays))


def grads_kernel(place, tile, ahead, first, gathered_ref, rate_ref, key_rows, value_rows, *refs):
    later = len(ahead)
    totals_ref, refs = (refs[later], refs[:later] + refs[later + 1 :]) if first else (None, refs)
    message_ref = refs[later]
    left_ref, back_ref, sems = refs[-3:]
    copies = started(refs[:later], refs[later + 1 : 2 * later + 1], ahead, sems)
    parties, rows, lanes = message_ref.shape
    width = gathered_ref.shape[2]
    share = width // parties
    count = key_rows.shape[0]
    section, block = place
    left_ref[...] = matrix(gathered_ref, 1, share).astype(f32).T.astype(bf16)
    gate, up = matrix(gathered_ref, 0, share), matrix(gathered_ref, 2, share)
    for start in range(0, count, tile):
        span = slice(start, start + tile)
        keys, values = key_rows[span, :], value_rows[span, :]
        rate = rate_ref[section, 0, block : block + 1, span]
        pre_gate = dot(gate, keys, NT)
        pre_up = dot(up, keys, NT)
        back = dot(left_ref[...], values, NT) * -rate
        sig = sigmoid(pre_gate)
        active = pre_gate * sig
        slope = sig + active * (1.0 - sig)
        back_ref[0, :, span] = (back * pre_up * slope).astype(bf16)
        back_ref[1, :, span] = (active * pre_up * rate).astype(bf16)
        back_ref[2, :, span] = (back * active).astype(bf16)
    keys, values = key_rows[...], value_rows[...]
    gradients = (
        dot(back_ref[0], keys, NN),
        -dot(back_ref[1], values, NN).T,
        dot(back_ref[2], keys, NN),
    )
    for index, gradient in enumerate(gradients):
        tiles = gradient.astype(bf16).reshape(parties, share, width)
        for half in range(width // lanes):
            start = (3 * half + index) * share
            message_ref[:, start : start + share, :] = tiles[
                :, :, half * lanes : (half + 1) * lanes
            ]
    used = 3 * share * (width // lanes)
    if rows > used:
        message_ref[:, used:, :] = jnp.broadcast_to(
            totals_ref[...][None], (parties, share, lanes)
        )
    for copy in copies:
        copy.wait()


def grads(gathered, rates, keys, values, place, ahead, totals=None):
    parties, _, width = gathered.shape
    share = width // parties
    count = keys.shape[0]
    if totals is not None:
        lanes = width // 2
        rows = 7 * share
    else:
        lanes = width
        rows = 3 * share
    return pl.pallas_call(
        functools.partial(grads_kernel, place, 256, [where for _, where in ahead], totals is not None),
        in_specs=[VMEM] * 4 + [HBM] * len(ahead) + [VMEM] * (totals is not None),
        out_specs=[VMEM] * (1 + len(ahead)),
        out_shape=[in_vmem(parties, rows, lanes, dtype=bf16)]
        + [rows_in_vmem(array) for array, _ in ahead],
        scratch_shapes=[
            pltpu.VMEM((width, width), bf16),
            pltpu.VMEM((3, width, count), bf16),
            pltpu.SemaphoreType.DMA((len(ahead),)),
        ],
        compiler_params=params(),
        cost_estimate=pl.CostEstimate(
            flops=12 * count * width * width, bytes_accessed=4 * count * width, transcendentals=0
        ),
        name="grads",
    )(gathered, rates, keys, values, *(in_hbm(array) for array, _ in ahead), *(() if totals is None else (totals,)))


def update_kernel(index, waits, *refs):
    arrived_ref, weights_ref, moment_ref = refs[:3]
    refs = refs[3:]
    rows = weights_ref.shape[0]
    halves = weights_ref.shape[1] // arrived_ref.shape[2]
    gradients = jnp.concatenate(
        [
            jnp.sum(arrived_ref[:, half * rows : (half + 1) * rows, :].astype(f32), axis=0)
            for half in range(halves)
        ],
        axis=1,
    )
    if index == 0:
        squares = jnp.sum(arrived_ref[:, halves * rows :, :].astype(f32), axis=0)
        squares = jnp.concatenate([squares] * halves, axis=1)
        refs[-1][...] = squares
    else:
        squares, refs = refs[0][...], refs[1:]
    square = squares[2 * index : 2 * index + 1, :] + squares[2 * index + 1 : 2 * index + 2, :]
    weights = weights_ref[...]
    moment = momentum_decay * moment_ref[...] + gradients * lax.rsqrt(square)
    stepped = weights - learn_rate * moment
    rescale = jnp.sqrt(
        jnp.sum(weights * weights, axis=1, keepdims=True)
        / (jnp.sum(stepped * stepped, axis=1, keepdims=True) + epsilon)
    )
    weights = stepped * rescale
    rounded = weights.astype(bf16)
    refs = refs[waits:]
    message_ref = refs[0]
    if len(message_ref.shape) == 3:
        message_ref[...] = jnp.broadcast_to(rounded[None], message_ref.shape)
        refs[1][...] = weights
        refs[2][...] = moment
    else:
        message_ref[:rows, :] = rounded
        message_ref[rows:, :] = moment.astype(bf16)


def update(index, arrived, weights, moment, squares, token, leaving):
    rows, width = weights.shape
    given, in_specs = [arrived, weights, moment], [VMEM] * 3
    if index > 0:
        given.append(squares)
        in_specs.append(VMEM)
    waits = token is not None
    if waits:
        given.append(token)
        in_specs.append(VMEM)
    if leaving:
        out_shape = [in_vmem(2 * rows, width, dtype=bf16)]
    else:
        out_shape = [in_vmem(arrived.shape[0], rows, width, dtype=bf16)]
        out_shape += [in_vmem(rows, width)] * 2
    if index == 0:
        out_shape.append(in_vmem(arrived.shape[1] - rows * width // arrived.shape[2], width))
    return pl.pallas_call(
        functools.partial(update_kernel, index, waits),
        in_specs=in_specs,
        out_specs=[VMEM] * len(out_shape),
        out_shape=out_shape,
        compiler_params=params(),
        name="update",
    )(*given)


def enter_kernel(
    first_ref,
    passed_ref,
    fresh_weights_ref,
    fresh_moment_ref,
    wait_ref,
    weights_ref,
    moment_ref,
    message_ref,
):
    rows = weights_ref.shape[0]
    first = first_ref[0] == 0
    passed = passed_ref[...].astype(f32)
    weights = jnp.where(first, fresh_weights_ref[...], passed[:rows])
    weights_ref[...] = weights
    moment_ref[...] = jnp.where(first, fresh_moment_ref[...], passed[rows:])
    message_ref[...] = jnp.broadcast_to(weights.astype(bf16)[None], message_ref.shape)


def enter(first, passed, fresh_weights, fresh_moment, token, parties):
    rows, width = fresh_weights.shape
    return pl.pallas_call(
        enter_kernel,
        in_specs=[SMEM] + [VMEM] * 4,
        out_specs=[VMEM] * 3,
        out_shape=[
            in_vmem(rows, width),
            in_vmem(rows, width),
            in_vmem(parties, rows, width, dtype=bf16),
        ],
        compiler_params=params(),
        name="enter",
    )(first, passed, fresh_weights, fresh_moment, token)


def apply_rows(place, parts, gathered, query_ref, query_rows, out_ref, held_ref, sems):
    length, width = query_rows.shape
    share = width // gathered.shape[0]
    if query_ref is not query_rows:
        (copy,) = started([query_ref], [query_rows], [place], sems)
        copy.wait()
    block = 256
    first = length if parts == 1 else -(-length // (parts * block)) * block
    copies = []
    for part, start in enumerate(range(0, length, first)):
        size = min(first, length - start)
        queries = query_rows[start : start + size, :]
        pre_gate = dot(queries, matrix(gathered, 0, share), NT)
        pre_up = dot(queries, matrix(gathered, 2, share), NT)
        hidden = (pre_gate * sigmoid(pre_gate) * pre_up).astype(bf16)
        held_ref[start : start + size, :] = dot(
            hidden, matrix(gathered, 1, share), NT
        ).astype(bf16)
        span = pl.ds(start, size)
        copies.append(
            pltpu.make_async_copy(
                held_ref.at[span, :], out_ref.at[*place].at[span, :], sems.at[1 + part]
            )
        )
        copies[-1].start()
    for copy in copies:
        copy.wait()


def apply_kernel(place, staged, waits, extra, when, aliased, hands, parts, gathered_ref, query_ref, *refs):
    wait_ref, refs = (refs[0], refs[1:]) if waits else (None, refs)
    extra_refs, refs = refs[: len(extra)], refs[len(extra) + aliased :]
    out_ref, query_rows, held_ref, sems = refs[0], *refs[-3:]
    if hands:
        refs[1][...] = wait_ref[...] if waits else jnp.zeros_like(refs[1])
    rows_ref = query_ref if staged else query_rows
    if extra == ("instead", "who"):
        gathered_ref = jnp.where(when(extra_refs[1][0]), extra_refs[0][...], gathered_ref[...])
    if extra == ("who",):

        @pl.when(when(extra_refs[0][0]))
        def _():
            apply_rows(place, parts, gathered_ref, query_ref, rows_ref, out_ref, held_ref, sems)

    else:
        apply_rows(place, parts, gathered_ref, query_ref, rows_ref, out_ref, held_ref, sems)


def apply_fast(
    gathered, queries, place, results, shape, token=None, parts=1, instead=None, who=None, when=None, hands=True
):
    count, width = shape[3:]
    staged = len(queries.shape) == 2
    waits = token is not None
    given = [gathered, queries if staged else in_hbm(queries)]
    in_specs = [VMEM, VMEM if staged else HBM]
    extra = ()
    if waits:
        given.append(token)
        in_specs.append(VMEM)
    if instead is not None:
        given.append(instead)
        in_specs.append(VMEM)
        extra += ("instead",)
    if who is not None:
        given.append(who)
        in_specs.append(SMEM)
        extra += ("who",)
    if results is not None:
        given.append(results)
        in_specs.append(HBM)
    out_shape = [jax.ShapeDtypeStruct(shape, bf16)]
    if hands:
        out_shape.append(in_vmem(*token.shape, dtype=token.dtype) if waits else TOKEN)
    results, *handed = pl.pallas_call(
        functools.partial(
            apply_kernel, place, staged, waits, extra, when, int(results is not None), hands, parts
        ),
        in_specs=in_specs,
        out_specs=[HBM] + [VMEM] * hands,
        out_shape=out_shape,
        input_output_aliases={} if results is None else {len(given) - 1: 0},
        scratch_shapes=[
            pltpu.VMEM((count, width), bf16),
            pltpu.VMEM((count, width), bf16),
            pltpu.SemaphoreType.DMA((1 + parts,)),
        ],
        compiler_params=params(),
        cost_estimate=pl.CostEstimate(
            flops=6 * count * width * width, bytes_accessed=4 * count * width, transcendentals=0
        ),
        name="apply",
    )(*given)
    return (results, *handed)


def exchanged(tiles):
    return lax.all_to_all(tiles, TOK, split_axis=0, concat_axis=0, tiled=True)


def passed_on(array):
    length = lax.axis_size("seg")
    return lax.ppermute(array, "seg", [(i, i + 1) for i in range(length - 1)])


def handed_back(array):
    length = lax.axis_size("seg")
    return lax.ppermute(array, "seg", [(i + 1, i) for i in range(length - 1)])


def gathered_by_last(is_last, state, rows, parties):
    width = state.shape[1]
    message = pl.pallas_call(
        copies_kernel,
        in_specs=[VMEM],
        out_specs=VMEM,
        out_shape=in_vmem(parties, rows, width, dtype=bf16),
        compiler_params=params(),
        name="copies",
    )(state)
    return lax.cond(is_last, exchanged, lambda tiles: tiles, message)


def columns_first(state):
    return jnp.swapaxes(state, 1, 2).reshape(-1, state.shape[1])


def rows_first(state, share):
    return jnp.swapaxes(state.reshape(-1, share, state.shape[1]), 1, 2)


def body(
    queries, key_vectors, values, token_rates, fast_weights, momenta, fresh_weights, fresh_momenta
):
    sections, _, blocks, count, _ = queries.shape
    parties = lax.axis_size(TOK)
    share = fast_weights.shape[3]
    place_in_chain = lax.axis_index("seg")
    who = place_in_chain.reshape(1)
    length = lax.axis_size("seg")
    is_last = place_in_chain == length - 1

    def early(segment):
        return (segment % 2 == 1) & (segment != length - 1)

    def late(segment):
        return (segment % 2 == 0) | (segment == length - 1)

    def at_end(segment):
        return segment == length - 1

    weights, moment = columns_first(fast_weights[0]), columns_first(momenta[0])
    fresh_weights, fresh_moment = columns_first(fresh_weights), columns_first(fresh_momenta)
    rows, shape = weights.shape[0], queries.shape
    places = [(section, 0, block) for section in range(sections) for block in range(blocks)]
    message, token = spread(weights, parties)
    *staged, totals = stage(token, who, token_rates, places[0], (key_vectors, values), share)
    gathered = exchanged(message)
    results = squares = owed = None
    pending = []
    for index, place in enumerate(places):
        last = index == len(places) - 1
        leaving = not last and place[2] == blocks - 1
        if last:
            ahead = ((queries, place),)
        else:
            ahead = ((key_vectors, places[index + 1]), (values, places[index + 1]))
        message, *staged = grads(
            gathered,
            token_rates,
            *staged,
            (place[0], place[2]),
            ahead,
            totals if index == 0 else None,
        )
        arrived = exchanged(message)
        token = None
        if pending and not leaving:
            results, token = apply_fast(*pending.pop(), results, shape, owed[0])
            owed = (handed_back(token), *owed[1:])
        message, *state = update(index, arrived, weights, moment, squares, token, leaving)
        if leaving:
            here = pending.pop()
            results, message = apply_fast(*here, results, shape, message, who=who, when=early)
            passed = passed_on(message)
            results, token = apply_fast(*here, results, shape, message, who=who, when=late)
            own = gathered_by_last(is_last, message, rows, parties)
            weights, moment, message = enter(
                who, passed, fresh_weights, fresh_moment, token, parties
            )
            gathered = exchanged(message)
            owed = (gathered, queries, place)
        else:
            weights, moment, squares = (*state, squares)[:3]
            gathered = exchanged(message)
            pending.append((gathered, queries, place))
    pending.pop()
    results, token = apply_fast(*owed, results, shape, weights, instead=own, who=who, when=at_end)
    (results,) = apply_fast(
        gathered, staged[0], places[-1], results, shape, token, parts=2, hands=False
    )
    return (results, rows_first(weights, share)[None], rows_first(moment, share)[None])


def solution(mesh):
    finer = Mesh(mesh.devices.reshape(mesh.shape["seg"], 4, 4), ("seg", "tok_0", "tok_1"))
    placed = (
        P(None, "seg", None, TOK, None),
        P(None, "seg", None, TOK, None),
        P(None, "seg", None, TOK, None),
        P(None, "seg", None, TOK),
        P("seg", None, None, TOK),
        P("seg", None, None, TOK),
        P(None, None, TOK),
        P(None, None, TOK),
    )
    return jax.shard_map(
        body,
        mesh=finer,
        in_specs=placed,
        out_specs=(
            P(None, "seg", None, TOK, None),
            P("seg", None, None, TOK),
            P("seg", None, None, TOK),
        ),
        check_vma=False,
    )
```
